256 devices in a mesh: gas: 16 (over z_hi, y), space: 16 (over x, z_lo, core).
Axes of the slice: x: 4, y: 4, z: 8 (z_hi: 4, z_lo: 2; z = z_hi * 2 + z_lo), core: 2. Of those that a mesh axis runs over, the one named last changes fastest.
Arguments:
- starting_kelvin_blocks: float32 [16, 2, 128, 128], P('space'), may hold values from 0.8 to 1.6
- volume_thermal_inertia: float32 [16, 2, 128, 128], P('space'), may hold values from 0.5 to 5
- volume_combustion_source: float32 [16, 2, 128, 128], P('space'), may hold values from 0.3 to 5
- extinction_coefficients: float32 [32, 16, 2, 128, 128], P('gas', 'space'), may hold values from 0.01 to 10, as said below
- blackbody_fractions: float32 [32, 16, 2, 128, 128], P('gas', 'space'), may hold values from 0.005 to 0.1
- earlier_irradiance: float32 [32, 16, 2, 128, 128], P('gas', 'space'), may hold values from 0.02 to 1
Outputs:
- final_temperature: float32 [16, 2, 128, 128], P('space')
- radiation: float32 [32, 16, 2, 128, 128], P('gas', 'space')
The draws below stay inside these ranges and needn't reach their ends.
Inputs may be any that keep to these rules, and one draw needn't show every extreme that they name: `extinction_coefficients`: gas g has a base rate 0.02 * 250^(g / 31), times a factor between 0.5 and 2 in each cell.
All inputs are finite; a program needn't handle non-finite values.
Results may differ from the reference program's by a relative error of at most 0.0001.
Values sent between devices are 32-bit elements; how exact they have to be, the bound alone decides.
No kernel may reach another device: no remote copies, remote signals or barrier semaphores. Data moves between devices by JAX's collectives and lax.ppermute only.
A program may use at most 64 MiB of HBM per device.

```python
import math
import jax
import jax.numpy as jnp
from jax import lax

BLOCK_WIDTH_EAST = 128
BLOCK_WIDTH_NORTH = 128
DEPTH_SLABS = 2
SWEEPS = 8
OUTER = 3
TY = 4
TX = 4
BLOCK_TOTAL = 16
GASES = 32


def draw_extinction_coefficients(key, part):
    dims_all = (GASES, BLOCK_TOTAL, DEPTH_SLABS, BLOCK_WIDTH_EAST, BLOCK_WIDTH_NORTH)
    gas_level = jnp.arange(GASES, dtype=jnp.float32) / max(GASES - 1, 1)
    base_rate = 0.02 * jnp.exp(gas_level * math.log(250.0))
    roughness = jnp.exp(jax.random.uniform(key, dims_all, jnp.float32, math.log(0.5), math.log(2.0)))
    return base_rate.reshape(GASES, 1, 1, 1, 1) * roughness


def shard_levels(rng, shape, split, low, top_value):
    factor_of, own = 1.0, jax.random.fold_in(rng, 6)
    for dim, blocks in split:
        draws = jnp.exp(jax.random.uniform(jax.random.fold_in(own, dim), (blocks,), jnp.float32, low / len(split), top_value / len(split)))
        factor_of = factor_of * jnp.repeat(draws, shape[dim] // blocks).reshape([-1 if axis == dim else 1 for axis in range(len(shape))])
    return factor_of


def setup_inputs(seed: int = 0) -> dict:
    key_of = jax.random.split(jax.random.key(seed), 7)
    return {
        "starting_kelvin_blocks": jnp.clip(0.8 + 0.8 * jax.random.uniform(key_of[0], (BLOCK_TOTAL, DEPTH_SLABS, BLOCK_WIDTH_EAST, BLOCK_WIDTH_NORTH), jnp.float32) ** shard_levels(key_of[0], (BLOCK_TOTAL, DEPTH_SLABS, BLOCK_WIDTH_EAST, BLOCK_WIDTH_NORTH), ((0, 16),), -0.2, 0.2), 0.8, 1.6),
        "volume_thermal_inertia": jnp.clip(jnp.exp(math.log(5.0) - 2.3025851 * jax.random.uniform(key_of[1], (BLOCK_TOTAL, DEPTH_SLABS, BLOCK_WIDTH_EAST, BLOCK_WIDTH_NORTH), jnp.float32) ** shard_levels(key_of[1], (BLOCK_TOTAL, DEPTH_SLABS, BLOCK_WIDTH_EAST, BLOCK_WIDTH_NORTH), ((0, 16),), -0.2, 0.2)), 0.5, 5.0),
        "volume_combustion_source": jnp.clip(jnp.exp(math.log(5.0) - 2.8134107 * jax.random.uniform(key_of[2], (BLOCK_TOTAL, DEPTH_SLABS, BLOCK_WIDTH_EAST, BLOCK_WIDTH_NORTH), jnp.float32) ** shard_levels(key_of[2], (BLOCK_TOTAL, DEPTH_SLABS, BLOCK_WIDTH_EAST, BLOCK_WIDTH_NORTH), ((0, 16),), -0.2, 0.2)), 0.3, 5.0),
        "extinction_coefficients": draw_extinction_coefficients(jax.random.fold_in(key_of[6], 71), 0),
        "blackbody_fractions": jnp.clip(jnp.exp(math.log(0.1) - 2.9957323 * jax.random.uniform(key_of[4], (GASES, BLOCK_TOTAL, DEPTH_SLABS, BLOCK_WIDTH_EAST, BLOCK_WIDTH_NORTH), jnp.float32) ** shard_levels(key_of[4], (GASES, BLOCK_TOTAL, DEPTH_SLABS, BLOCK_WIDTH_EAST, BLOCK_WIDTH_NORTH), ((0, 16), (1, 16)), -0.2, 0.2)), 0.005, 0.1),
        "earlier_irradiance": jnp.clip(jnp.exp(math.log(1.0) - 3.912023 * jax.random.uniform(key_of[5], (GASES, BLOCK_TOTAL, DEPTH_SLABS, BLOCK_WIDTH_EAST, BLOCK_WIDTH_NORTH), jnp.float32) ** shard_levels(key_of[5], (GASES, BLOCK_TOTAL, DEPTH_SLABS, BLOCK_WIDTH_EAST, BLOCK_WIDTH_NORTH), ((0, 16), (1, 16)), -0.2, 0.2)), 0.02, 1.0),
    }


LOW_BOUND = 0.05
HIGH_BOUND = 2.0


def sweep_factors(count):
    theta_mid = (HIGH_BOUND + LOW_BOUND) / 2.0
    delta_half = (HIGH_BOUND - LOW_BOUND) / 2.0
    sigma_ratio = theta_mid / delta_half
    rho_now = 1.0 / sigma_ratio
    factors = []
    for sweep_num in range(count):
        rho_next = 1.0 / (2.0 * sigma_ratio - rho_now)
        factors.append((rho_next * rho_now, 2.0 * rho_next / delta_half))
        rho_now = rho_next
    return theta_mid, factors


def blocks_to_mesh(field):
    count = field.shape[0]
    blocks = field.reshape(count, TX, TY, DEPTH_SLABS, BLOCK_WIDTH_EAST, BLOCK_WIDTH_NORTH)
    return blocks.transpose(0, 3, 1, 4, 2, 5).reshape(count, DEPTH_SLABS, TX * BLOCK_WIDTH_EAST, TY * BLOCK_WIDTH_NORTH)


def to_tiles(field):
    count = field.shape[0]
    blocks = field.reshape(count, DEPTH_SLABS, TX, BLOCK_WIDTH_EAST, TY, BLOCK_WIDTH_NORTH)
    return blocks.transpose(0, 2, 4, 1, 3, 5).reshape(count, TX * TY, DEPTH_SLABS, BLOCK_WIDTH_EAST, BLOCK_WIDTH_NORTH)


def neighbours(field):
    padded = jnp.pad(field, 1)
    return [padded[:-2, 1:-1, 1:-1], padded[2:, 1:-1, 1:-1],
            padded[1:-1, :-2, 1:-1], padded[1:-1, 2:, 1:-1],
            padded[1:-1, 1:-1, :-2], padded[1:-1, 1:-1, 2:]]


def coefficients(absorb):
    couplings = [2.0 / (3.0 * (absorb + other)) for other in neighbours(absorb)]
    diagonal = absorb
    for coupling in couplings:
        diagonal = diagonal + coupling
    return couplings, diagonal


def operate(field, couplings, diagonal):
    total = diagonal * field
    for coupling, other in zip(couplings, neighbours(field)):
        total = total - coupling * other
    return total


def solve_gas(absorb, weight, start, fourth):
    couplings, diagonal = coefficients(absorb)
    theta_mid, factors = sweep_factors(SWEEPS - 1)
    source = 4.0 * absorb * weight * fourth
    iterate = start
    scaled_res = (source - operate(iterate, couplings, diagonal)) / diagonal
    direction = scaled_res / theta_mid
    for sweep_num in range(SWEEPS):
        iterate = iterate + direction
        if sweep_num < SWEEPS - 1:
            scaled_res = scaled_res - operate(direction, couplings, diagonal) / diagonal
            keep_part, push_part = factors[sweep_num]
            direction = keep_part * direction + push_part * scaled_res
    return iterate


def linearized_correction(current_kelvin, earlier_kelvin, thermal_inertia, combustion_source, emitted_power, taken_energy):
    balance_mismatch = thermal_inertia * (current_kelvin - earlier_kelvin) + 4.0 * emitted_power * current_kelvin ** 4 - taken_energy - combustion_source
    return current_kelvin - balance_mismatch / (thermal_inertia + 16.0 * emitted_power * current_kelvin ** 3)


def reference(starting_kelvin_blocks, volume_thermal_inertia, volume_combustion_source, extinction_coefficients, blackbody_fractions, earlier_irradiance):
    absorb_all = blocks_to_mesh(extinction_coefficients)
    weight_all = blocks_to_mesh(blackbody_fractions)
    iterate_all = blocks_to_mesh(earlier_irradiance)
    earlier_kelvin = blocks_to_mesh(starting_kelvin_blocks[None])[0]
    thermal_inertia = blocks_to_mesh(volume_thermal_inertia[None])[0]
    combustion_source = blocks_to_mesh(volume_combustion_source[None])[0]
    emitted_power = jnp.sum(absorb_all * weight_all, axis=0)
    current_kelvin = earlier_kelvin
    for outer_step in range(OUTER):
        fourth = current_kelvin ** 4

        def one_gas(items):
            return solve_gas(items[0], items[1], items[2], fourth)

        iterate_all = lax.map(one_gas, (absorb_all, weight_all, iterate_all))
        taken_energy = jnp.sum(absorb_all * iterate_all, axis=0)
        current_kelvin = linearized_correction(current_kelvin, earlier_kelvin, thermal_inertia, combustion_source, emitted_power, taken_energy)
    return to_tiles(current_kelvin[None])[0], to_tiles(iterate_all)
```

```python
import functools

import jax
import jax.numpy as jnp
from jax import lax
from jax.experimental import pallas as pl
from jax.experimental.pallas import tpu as pltpu
from jax.sharding import PartitionSpec as P

SWEEPS = 8
OUTER = 3
LOW_BOUND = 0.05
HIGH_BOUND = 2.0

TILE = 128
HALO = SWEEPS * OUTER
ROWS = TILE + 2 * HALO
PAD = 8
STEP = 16
PLANES = 18
PACK = 5
PACKS = 4
CHUNK = 40
GROUP = 16
LAST = ROWS // 8 - 1
EXTRA = (1, 2, LAST - 2, LAST - 1)
VMEM_LIMIT = 40 * 1024 * 1024
F32 = jnp.float32


def sweep_weights():
    theta_mid = (HIGH_BOUND + LOW_BOUND) / 2.0
    delta_half = (HIGH_BOUND - LOW_BOUND) / 2.0
    sigma_ratio = theta_mid / delta_half
    rho_now = 1.0 / sigma_ratio
    weights = [(0.0, 1.0 / theta_mid)]
    for _ in range(SWEEPS - 1):
        rho_next = 1.0 / (2.0 * sigma_ratio - rho_now)
        weights.append((rho_next * rho_now, 2.0 * rho_next / delta_half))
        rho_now = rho_next
    return weights


def own_planes(refs):
    k, w, g, t, i, s = refs
    planes = [(ref, (gas, 0, z)) for ref in (k, w, g) for gas in range(2) for z in range(2)]
    return planes + [(ref, (0, z)) for ref in (t, i, s) for z in range(2)]


def pack_x_kernel(*refs):
    up, down = refs[6:]
    for p, (ref, at) in enumerate(own_planes(refs[:6])):
        up[p] = ref[at + (pl.ds(TILE - HALO, HALO), slice(None))]
        down[p] = ref[at + (pl.ds(0, HALO), slice(None))]


def row_parts():
    parts = [(0, HALO, "top", 0)]
    parts += [(HALO + r, 32, "own", r) for r in range(0, TILE, 32)]
    parts += [(HALO + TILE, HALO, "bottom", 0)]
    return parts


def pack_y_kernel(*refs):
    planes = own_planes(refs[:6])
    top, bottom, right, left = refs[6:]
    for row, count, kind, at_row in row_parts():
        lane = lax.broadcasted_iota(jnp.int32, (count, TILE), 1)
        for t in range(PACKS):
            to_right = jnp.zeros((count, TILE), F32)
            to_left = jnp.zeros((count, TILE), F32)
            for j in range(PACK):
                p = t * PACK + j
                if p >= PLANES:
                    break
                if kind == "own":
                    ref, at = planes[p]
                    value = ref[at + (pl.ds(at_row, count), slice(None))]
                else:
                    value = (top if kind == "top" else bottom)[p]
                here = (lane >= HALO * j) & (lane < HALO * (j + 1))
                to_left = jnp.where(here, pltpu.roll(value, (HALO * j) % TILE, 1), to_left)
                to_right = jnp.where(here, pltpu.roll(value, (HALO * (j + 1)) % TILE, 1), to_right)
            right[t, pl.ds(row, count), :] = to_right
            left[t, pl.ds(row, count), :] = to_left


def chunk_out(out, field, first=0):
    for c in range(GROUP):
        z, i = divmod(c, 8)
        for l in range(2):
            out[c, pl.ds(first + 16 * l, 16), :] = field[z, l, pl.ds(HALO + 16 * i, 16), :]
        e, l, z = c // 4, (c // 2) % 2, c % 2
        out[c, pl.ds(first + 32, 8), :] = field[z, l, pl.ds(8 * EXTRA[e], 8), :]


def chunk_in(field, chunks, change):
    for c in range(GROUP):
        z, i = divmod(c, 8)
        for l in range(2):
            field[z, l, pl.ds(HALO + 16 * i, 16), :] = change(chunks[c, pl.ds(16 * l, 16), :])
        e, l, z = c // 4, (c // 2) % 2, c % 2
        field[z, l, pl.ds(8 * EXTRA[e], 8), :] = change(chunks[c, pl.ds(32, 8), :])


def fourth(value):
    square = value * value
    return square * square


def left_right(own, other, lane):
    left = pltpu.roll(jnp.where(lane == TILE - 1, other, own), 1, 1)
    right = pltpu.roll(jnp.where(lane == 0, other, own), TILE - 1, 1)
    return left, right


def each_step(first, last, body):
    def run(i, carry):
        body(pl.multiple_of(first + STEP * i, 8))
        return carry

    lax.fori_loop(0, (last - first) // STEP, run, 0)


def solve(step, a, q, t4, sp, now, old):
    first, last = 8 * step, ROWS - 8 * step

    def source(r):
        for gz in range(4):
            for l in range(2):
                weight = q[gz, l, pl.ds(r, STEP), :]
                value = weight * t4[gz % 2, l, pl.ds(r, STEP), :]
                sp[gz, l, pl.ds(r, STEP), :] = jnp.where(weight > 0.0, value, 0.0)

    each_step(first, last, source)
    for sweep, (keep, push) in enumerate(sweep_weights()):
        src, dst = (now, old) if sweep % 2 == 0 else (old, now)

        def body(r, src=src, dst=dst, keep=keep, push=push, sweep=sweep):
            lane = lax.broadcasted_iota(jnp.int32, (STEP, TILE), 1)
            rows = pl.ds(r, STEP)
            for g in range(2):
                own = [[src[2 * g + z, l, pl.ds(r + PAD, STEP), :] for l in range(2)] for z in range(2)]
                for z in range(2):
                    for l in range(2):
                        gz = 2 * g + z
                        here = own[z][l]
                        left, right = left_right(here, own[z][1 - l], lane)
                        total = sp[gz, l, rows, :] + a[0, gz, l, rows, :] * own[1 - z][l]
                        total += a[1, gz, l, rows, :] * src[gz, l, pl.ds(r + PAD - 1, STEP), :]
                        total += a[2, gz, l, rows, :] * src[gz, l, pl.ds(r + PAD + 1, STEP), :]
                        total += a[3, gz, l, rows, :] * left + a[4, gz, l, rows, :] * right
                        value = (1.0 + keep - push) * here + push * total
                        if sweep:
                            value -= keep * dst[gz, l, pl.ds(r + PAD, STEP), :]
                        dst[gz, l, pl.ds(r + PAD, STEP), :] = value

        each_step(first, last, body)


def absorb(kap, now, out):
    def body(r):
        for z in range(2):
            for l in range(2):
                rows = pl.ds(r + PAD, STEP)
                out[z, l, pl.ds(r, STEP), :] = (
                    kap[z, l, rows, :] * now[z, l, rows, :] + kap[2 + z, l, rows, :] * now[2 + z, l, rows, :]
                )

    each_step(8, ROWS - 8, body)


def first_kernel(*refs):
    planes = own_planes(refs[:6])
    top, bottom, from_left, from_right = refs[6:10]
    a, q, kap, now, sums, held = refs[10:16]
    tis, sp, t4, old = refs[16:]
    planck = sp

    def place(p):
        if p < 4:
            return kap, p, PAD
        if p < 8:
            return q, p - 4, 0
        if p < 12:
            return now, p - 8, PAD
        return tis, p - 12, 0

    for p in range(PLANES):
        dst, at, pad = place(p)
        ref, own = planes[p]
        dst[at, 0, pl.ds(pad, HALO), :] = top[p]
        dst[at, 0, pl.ds(pad + HALO, TILE), :] = ref[own]
        dst[at, 0, pl.ds(pad + HALO + TILE, HALO), :] = bottom[p]
    for buffer in (kap, now, old):
        for gz in range(4):
            for l in range(2):
                buffer[gz, l, pl.ds(0, PAD), :] = jnp.zeros((PAD, TILE), F32)
                buffer[gz, l, pl.ds(PAD + ROWS, PAD), :] = jnp.zeros((PAD, TILE), F32)

    def sides(r):
        lane = lax.broadcasted_iota(jnp.int32, (STEP, TILE), 1)
        for t in range(PACKS):
            lefts = from_left[t, pl.ds(r, STEP), :]
            rights = from_right[t, pl.ds(r, STEP), :]
            for j in range(PACK):
                p = t * PACK + j
                if p >= PLANES:
                    break
                dst, at, pad = place(p)
                right = jnp.where(lane < HALO, pltpu.roll(rights, (TILE - HALO * j) % TILE, 1), 0.0)
                left = pltpu.roll(lefts, (TILE - HALO * (j + 1)) % TILE, 1)
                dst[at, 1, pl.ds(r + pad, STEP), :] = jnp.where(lane >= TILE - HALO, left, right)

    each_step(0, ROWS, sides)
    for f in range(3):
        chunk_out(held.at[f], tis.at[pl.ds(2 * f, 2)])

    def coefficients(r):
        lane = lax.broadcasted_iota(jnp.int32, (STEP, TILE), 1)
        rows = pl.ds(r, STEP)
        two_thirds = 2.0 / 3.0
        for z in range(2):
            for l in range(2):
                t4[z, l, rows, :] = fourth(tis[z, l, rows, :])
                planck[z, l, rows, :] = (
                    kap[z, l, pl.ds(r + PAD, STEP), :] * q[z, l, rows, :]
                    + kap[2 + z, l, pl.ds(r + PAD, STEP), :] * q[2 + z, l, rows, :]
                )
        for g in range(2):
            own = [[kap[2 * g + z, l, pl.ds(r + PAD, STEP), :] for l in range(2)] for z in range(2)]
            between = [two_thirds / (own[0][l] + own[1][l]) for l in range(2)]
            for z in range(2):
                for l in range(2):
                    gz = 2 * g + z
                    here = own[z][l]
                    left, right = left_right(here, own[z][1 - l], lane)
                    couplings = [
                        between[l],
                        two_thirds / (here + kap[gz, l, pl.ds(r + PAD - 1, STEP), :]),
                        two_thirds / (here + kap[gz, l, pl.ds(r + PAD + 1, STEP), :]),
                        two_thirds / (here + left),
                        two_thirds / (here + right),
                    ]
                    diagonal = here + two_thirds / here
                    for coupling in couplings:
                        diagonal += coupling
                    inside = here > 0.0
                    inverse = 1.0 / diagonal
                    for f, coupling in enumerate(couplings):
                        a[f, gz, l, rows, :] = jnp.where(inside, coupling * inverse, 0.0)
                    weight = 4.0 * here * q[gz, l, rows, :] * inverse
                    q[gz, l, rows, :] = jnp.where(inside, weight, 0.0)

    each_step(0, ROWS, coefficients)
    chunk_out(sums, planck, CHUNK)
    solve(0, a, q, t4, sp, now, old)
    absorb(kap, now, t4)
    chunk_out(sums, t4)


def next_kernel(a, q, kap, now_in, chunks, now, sums, sp, t4, old):
    now[...] = now_in[...]
    chunk_in(t4, chunks, fourth)
    solve(1, a, q, t4, sp, now, old)
    absorb(kap, now, t4)
    chunk_out(sums, t4)


def last_kernel(a, q, kap, now_in, chunks, radiation, sums, sp, t4, old, now):
    now[...] = now_in[...]
    chunk_in(t4, chunks, fourth)
    solve(2, a, q, t4, sp, now, old)
    rows = pl.ds(PAD + HALO, TILE)
    for gz in range(4):
        radiation[gz // 2, 0, gz % 2, :, :] = now[gz, 0, rows, :]
    for c in range(GROUP):
        z, i = divmod(c, 8)
        part = pl.ds(PAD + HALO + 16 * i, 16)
        sums[c] = kap[z, 0, part, :] * now[z, 0, part, :] + kap[2 + z, 0, part, :] * now[2 + z, 0, part, :]


def corrected(current, earlier, inertia, source, emitted, taken):
    mismatch = inertia * (current - earlier) + 4.0 * emitted * fourth(current) - taken - source
    slope = inertia + 16.0 * emitted * (current * current * current)
    return jnp.where(inertia > 0.0, current - mismatch / slope, 0.0)


def first_update(me, parts, held, everyone, state):
    total = parts[0]
    for c in range(1, GROUP):
        total += parts[c]
    taken, emitted = total[:CHUNK], total[CHUNK:]
    earlier, inertia, source = held[0, me[0]], held[1, me[0]], held[2, me[0]]
    current = corrected(earlier, earlier, inertia, source, emitted, taken)
    for f, value in enumerate((current, earlier, inertia, source, emitted)):
        state[f] = value
    for c in range(GROUP):
        everyone[c] = current


def next_update(parts, state_in, everyone, state):
    count = everyone.shape[1]
    total = parts[0]
    for c in range(1, GROUP):
        total += parts[c]
    current, earlier, inertia, source, emitted = (state_in[f, pl.ds(0, count), :] for f in range(5))
    current = corrected(current, earlier, inertia, source, emitted, total)
    if state is not None:
        for f, value in enumerate((current, earlier, inertia, source, emitted)):
            state[f] = value
    for c in range(GROUP):
        everyone[c] = current


def last_update(parts, state_in, everyone):
    next_update(parts, state_in, everyone, None)


def call(kernel, outs, scratch=(), smem=0):
    def shape(*dims):
        return jax.ShapeDtypeStruct(dims, F32)

    def run(*args):
        specs = [pl.BlockSpec(memory_space=pltpu.SMEM)] * smem
        specs += [pl.BlockSpec(memory_space=pltpu.VMEM)] * (len(args) - smem)
        return pl.pallas_call(
            kernel,
            out_shape=[shape(*dims) for dims in outs],
            in_specs=specs,
            out_specs=[pl.BlockSpec(memory_space=pltpu.VMEM)] * len(outs),
            scratch_shapes=[pltpu.VMEM(dims, F32) for dims in scratch],
            compiler_params=pltpu.CompilerParams(vmem_limit_bytes=VMEM_LIMIT),
        )(*args)

    return run


FIELD = (4, 2, ROWS, TILE)
PADDED = (4, 2, ROWS + 2 * PAD, TILE)
SHARED = (2, 2, ROWS, TILE)


def swap(array):
    return lax.all_to_all(array, "gas", 0, 0)


def on_device(*inputs):
    kelvin, inertia, source, extinction, fractions, irradiance = inputs
    own = (extinction, fractions, irradiance, kelvin, inertia, source)
    devices = lax.axis_size("space")
    across = 4
    up, down = call(pack_x_kernel, [(PLANES, HALO, TILE)] * 2)(*own)
    top = lax.ppermute(up, "space", [(i, i + across) for i in range(devices - across)])
    bottom = lax.ppermute(down, "space", [(i + across, i) for i in range(devices - across)])
    right, left = call(pack_y_kernel, [(PACKS, ROWS, TILE)] * 2)(*own, top, bottom)
    pairs = [(i, i + 1) for i in range(devices) if i % across != across - 1]
    from_left = lax.ppermute(right, "space", pairs)
    from_right = lax.ppermute(left, "space", [(j, i) for i, j in pairs])
    a, q, kap, now, sums, held = call(
        first_kernel,
        [(5,) + FIELD, FIELD, PADDED, PADDED, (GROUP, 2 * CHUNK, TILE), (3, GROUP, CHUNK, TILE)],
        [(6, 2, ROWS, TILE), FIELD, SHARED, PADDED],
    )(*own, top, bottom, from_left, from_right)
    me = lax.axis_index("gas").reshape(1)
    chunks, state = call(first_update, [(GROUP, CHUNK, TILE), (5, CHUNK, TILE)], smem=1)(me, swap(sums), held)
    now, sums = call(next_kernel, [PADDED, (GROUP, CHUNK, TILE)], [FIELD, SHARED, PADDED])(
        a, q, kap, now, swap(chunks)
    )
    chunks, state = call(next_update, [(GROUP, CHUNK, TILE), (5, CHUNK, TILE)])(swap(sums), state)
    radiation, sums = call(
        last_kernel, [(2, 1, 2, TILE, TILE), (GROUP, 16, TILE)], [FIELD, SHARED, PADDED, PADDED]
    )(a, q, kap, now, swap(chunks))
    (chunks,) = call(last_update, [(GROUP, 16, TILE)])(swap(sums), state)
    final = swap(chunks).reshape(1, 2, TILE, TILE)
    return final, radiation


def solution(mesh):
    placed = (
        P("space", None, None, None),
        P("space", None, None, None),
        P("space", None, None, None),
        P("gas", "space", None, None, None),
        P("gas", "space", None, None, None),
        P("gas", "space", None, None, None),
    )
    return jax.shard_map(
        on_device,
        mesh=mesh,
        in_specs=placed,
        out_specs=(P("space", None, None, None), P("gas", "space", None, None, None)),
        check_vma=False,
    )
```

```python
import functools

import jax
import jax.numpy as jnp
from jax import lax
from jax.experimental import pallas as pl
from jax.experimental.pallas import tpu as pltpu
from jax.sharding import PartitionSpec as P

SWEEPS = 8
OUTER = 3
LOW_BOUND = 0.05
HIGH_BOUND = 2.0

TILE = 128
HALO = SWEEPS * OUTER
ROWS = TILE + 2 * HALO
PAD = 8
STEP = 16
PLANES = 18
PACK = 5
PACKS = 4
RING = 4
MAIN = 64
FULL = 80
CHUNK = 104
SIDE = 16
VMEM_LIMIT = 16 * 1024 * 1024
F32 = jnp.float32


def sweep_weights():
    theta_mid = (HIGH_BOUND + LOW_BOUND) / 2.0
    delta_half = (HIGH_BOUND - LOW_BOUND) / 2.0
    sigma_ratio = theta_mid / delta_half
    rho_now = 1.0 / sigma_ratio
    weights = [(0.0, 1.0 / theta_mid)]
    for _ in range(SWEEPS - 1):
        rho_next = 1.0 / (2.0 * sigma_ratio - rho_now)
        weights.append((rho_next * rho_now, 2.0 * rho_next / delta_half))
        rho_now = rho_next
    return weights


def load_kernel(*refs):
    planes, up, down, sems = refs[6:]
    copies = []
    for f, ref in enumerate(refs[:6]):
        for gas in range(2 if f < 3 else 1):
            first = 4 * f + 2 * gas if f < 3 else 12 + 2 * (f - 3)
            source = ref.at[gas, 0] if f < 3 else ref.at[0]
            for row, count, out in ((TILE - HALO, HALO, up), (0, HALO, down), (0, TILE, planes)):
                copies.append(
                    pltpu.make_async_copy(
                        source.at[:, pl.ds(row, count), :], out.at[pl.ds(first, 2)], sems.at[len(copies)]
                    )
                )
    for copy in copies:
        copy.start()
    for copy in copies:
        copy.wait()


def row_parts():
    parts = [(0, HALO, "top", 0)]
    parts += [(HALO + r, 32, "own", r) for r in range(0, TILE, 32)]
    parts += [(HALO + TILE, HALO, "bottom", 0)]
    return parts


def pack_y_kernel(planes, top, bottom, right, left):
    for row, count, kind, at_row in row_parts():
        lane = lax.broadcasted_iota(jnp.int32, (count, TILE), 1)
        for t in range(PACKS):
            to_right = jnp.zeros((count, TILE), F32)
            to_left = jnp.zeros((count, TILE), F32)
            for j in range(PACK):
                p = t * PACK + j
                if p >= PLANES:
                    break
                if kind == "own":
                    value = planes[p, pl.ds(at_row, count), :]
                else:
                    value = (top if kind == "top" else bottom)[p]
                here = (lane >= HALO * j) & (lane < HALO * (j + 1))
                to_left = jnp.where(here, pltpu.roll(value, (HALO * j) % TILE, 1), to_left)
                to_right = jnp.where(here, pltpu.roll(value, (HALO * (j + 1)) % TILE, 1), to_right)
            right[t, pl.ds(row, count), :] = to_right
            left[t, pl.ds(row, count), :] = to_left


def chunk_rows(half):
    return [HALO + MAIN * half + 8 * k for k in range(8)] + ([8, 16], [ROWS - 24, ROWS - 16])[half]


def chunk_out(out, field, first=0):
    lane = lax.broadcasted_iota(jnp.int32, (8, TILE), 1)
    for c in range(RING):
        z, rows = c // 2, chunk_rows(c % 2)
        for k, row in enumerate(rows):
            out[c, pl.ds(first + 8 * k, 8), :] = field[z, 0, pl.ds(row, 8), :]
        for slot in range(3):
            packed = jnp.zeros((8, TILE), F32)
            for j, k in enumerate(range(slot, 10, 3)):
                value = pltpu.roll(field[z, 1, pl.ds(rows[k], 8), :], (SIDE + 32 * j) % TILE, 1)
                packed = jnp.where((lane >= 32 * j) & (lane < 32 * (j + 1)), value, packed)
            out[c, pl.ds(first + FULL + 8 * slot, 8), :] = packed


def chunk_in(field, chunks, change):
    for c in range(RING):
        z, rows = c // 2, chunk_rows(c % 2)
        for k, row in enumerate(rows):
            field[z, 0, pl.ds(row, 8), :] = change(chunks[c, pl.ds(8 * k, 8), :])
            packed = change(chunks[c, pl.ds(FULL + 8 * (k % 3), 8), :])
            field[z, 1, pl.ds(row, 8), :] = pltpu.roll(packed, (TILE - SIDE - 32 * (k // 3)) % TILE, 1)


def turn(me, k):
    return lax.rem(me[0] + k, RING)


def send_chunks(me, chunks, outs):
    for k, out in enumerate(outs):
        out[...] = chunks[turn(me, k)]


def gather_chunks(me, chunks, parts):
    for k, part in enumerate(parts):
        chunks[turn(me, RING - k)] = part[...]


def fourth(value):
    square = value * value
    return square * square


def left_right(own, other, lane):
    left = pltpu.roll(jnp.where(lane == TILE - 1, other, own), 1, 1)
    right = pltpu.roll(jnp.where(lane == 0, other, own), TILE - 1, 1)
    return left, right


def each_step(first, last, body):
    for r in range(first, last, STEP):
        body(r)


def solve(step, a, q, t4, sp, start, now, old):
    first, last = 8 * step, ROWS - 8 * step

    def source(r):
        for gz in range(4):
            for l in range(2):
                weight = q[gz, l, pl.ds(r, STEP), :]
                value = weight * t4[gz % 2, l, pl.ds(r, STEP), :]
                sp[gz, l, pl.ds(r, STEP), :] = jnp.where(weight > 0.0, value, 0.0)

    each_step(first, last, source)
    before, src = None, start
    for sweep, (keep, push) in enumerate(sweep_weights()):
        dst = old if sweep % 2 == 0 else now

        def body(r, src=src, dst=dst, before=before, keep=keep, push=push):
            lane = lax.broadcasted_iota(jnp.int32, (STEP, TILE), 1)
            rows = pl.ds(r, STEP)
            for g in range(2):
                own = [[src[2 * g + z, l, pl.ds(r + PAD, STEP), :] for l in range(2)] for z in range(2)]
                for z in range(2):
                    for l in range(2):
                        gz = 2 * g + z
                        here = own[z][l]
                        left, right = left_right(here, own[z][1 - l], lane)
                        total = sp[gz, l, rows, :] + a[0, gz, l, rows, :] * own[1 - z][l]
                        total += a[1, gz, l, rows, :] * src[gz, l, pl.ds(r + PAD - 1, STEP), :]
                        total += a[2, gz, l, rows, :] * src[gz, l, pl.ds(r + PAD + 1, STEP), :]
                        total += a[3, gz, l, rows, :] * left + a[4, gz, l, rows, :] * right
                        value = (1.0 + keep - push) * here + push * total
                        if before is not None:
                            value -= keep * before[gz, l, pl.ds(r + PAD, STEP), :]
                        dst[gz, l, pl.ds(r + PAD, STEP), :] = value

        each_step(first, last, body)
        before, src = src, dst


def absorb(kap, now, out):
    def body(r):
        for z in range(2):
            for l in range(2):
                rows = pl.ds(r + PAD, STEP)
                out[z, l, pl.ds(r, STEP), :] = (
                    kap[z, l, rows, :] * now[z, l, rows, :] + kap[2 + z, l, rows, :] * now[2 + z, l, rows, :]
                )

    each_step(8, ROWS - 8, body)


def first_kernel(*refs):
    planes, top, bottom, from_left, from_right, me = refs[:6]
    a, q, kap, now, held, *outs = refs[6 : 11 + RING]
    tis, sp, t4, old, begin, sums = refs[11 + RING :]
    planck = sp

    def place(p):
        if p < 4:
            return kap, p, PAD
        if p < 8:
            return q, p - 4, 0
        if p < 12:
            return begin, p - 8, PAD
        return tis, p - 12, 0

    for p in range(PLANES):
        dst, at, pad = place(p)
        dst[at, 0, pl.ds(pad, HALO), :] = top[p]
        dst[at, 0, pl.ds(pad + HALO, TILE), :] = planes[p]
        dst[at, 0, pl.ds(pad + HALO + TILE, HALO), :] = bottom[p]
    def sides(r):
        lane = lax.broadcasted_iota(jnp.int32, (STEP, TILE), 1)
        for t in range(PACKS):
            lefts = from_left[t, pl.ds(r, STEP), :]
            rights = from_right[t, pl.ds(r, STEP), :]
            for j in range(PACK):
                p = t * PACK + j
                if p >= PLANES:
                    break
                dst, at, pad = place(p)
                right = jnp.where(lane < HALO, pltpu.roll(rights, (TILE - HALO * j) % TILE, 1), 0.0)
                left = pltpu.roll(lefts, (TILE - HALO * (j + 1)) % TILE, 1)
                dst[at, 1, pl.ds(r + pad, STEP), :] = jnp.where(lane >= TILE - HALO, left, right)

    each_step(0, ROWS, sides)
    for f in range(3):
        chunk_out(sums, tis.at[pl.ds(2 * f, 2)])
        held[f] = sums[me[0], pl.ds(0, CHUNK), :]

    def coefficients(r):
        lane = lax.broadcasted_iota(jnp.int32, (STEP, TILE), 1)
        rows = pl.ds(r, STEP)
        two_thirds = 2.0 / 3.0
        for z in range(2):
            for l in range(2):
                t4[z, l, rows, :] = fourth(tis[z, l, rows, :])
                planck[z, l, rows, :] = (
                    kap[z, l, pl.ds(r + PAD, STEP), :] * q[z, l, rows, :]
                    + kap[2 + z, l, pl.ds(r + PAD, STEP), :] * q[2 + z, l, rows, :]
                )
        for g in range(2):
            own = [[kap[2 * g + z, l, pl.ds(r + PAD, STEP), :] for l in range(2)] for z in range(2)]
            between = [two_thirds / (own[0][l] + own[1][l]) for l in range(2)]
            for z in range(2):
                for l in range(2):
                    gz = 2 * g + z
                    here = own[z][l]
                    left, right = left_right(here, own[z][1 - l], lane)
                    couplings = [
                        between[l],
                        two_thirds / (here + kap[gz, l, pl.ds(r + PAD - 1, STEP), :]),
                        two_thirds / (here + kap[gz, l, pl.ds(r + PAD + 1, STEP), :]),
                        two_thirds / (here + left),
                        two_thirds / (here + right),
                    ]
                    diagonal = here + two_thirds / here
                    for coupling in couplings:
                        diagonal += coupling
                    inside = here > 0.0
                    inverse = 1.0 / diagonal
                    for f, coupling in enumerate(couplings):
                        a[f, gz, l, rows, :] = jnp.where(inside, coupling * inverse, 0.0)
                    weight = 4.0 * here * q[gz, l, rows, :] * inverse
                    q[gz, l, rows, :] = jnp.where(inside, weight, 0.0)

    each_step(0, ROWS, coefficients)
    chunk_out(sums, planck, CHUNK)
    solve(0, a, q, t4, sp, begin, now, old)
    absorb(kap, now, t4)
    chunk_out(sums, t4)
    send_chunks(me, sums, outs)


def next_kernel(a, q, kap, start, *refs):
    parts, me = refs[:RING], refs[RING]
    now, *outs = refs[RING + 1 : 2 * RING + 2]
    sp, t4, old, sums = refs[2 * RING + 2 :]
    gather_chunks(me, sums, parts)
    chunk_in(t4, sums, fourth)
    solve(1, a, q, t4, sp, start, now, old)
    absorb(kap, now, t4)
    chunk_out(sums, t4)
    send_chunks(me, sums, outs)


def last_kernel(a, q, kap, start, *refs):
    parts, me = refs[:RING], refs[RING]
    radiation, *outs = refs[RING + 1 : 2 * RING + 2]
    sp, t4, old, now, sums = refs[2 * RING + 2 :]
    gather_chunks(me, sums, parts)
    chunk_in(t4, sums, fourth)
    solve(2, a, q, t4, sp, start, now, old)
    rows = pl.ds(PAD + HALO, TILE)
    for gz in range(4):
        radiation[gz // 2, 0, gz % 2, :, :] = now[gz, 0, rows, :]
    for c in range(RING):
        z = c // 2
        part = pl.ds(PAD + HALO + MAIN * (c % 2), MAIN)
        sums[c, pl.ds(0, MAIN), :] = (
            kap[z, 0, part, :] * now[z, 0, part, :] + kap[2 + z, 0, part, :] * now[2 + z, 0, part, :]
        )
    for k, out in enumerate(outs):
        out[...] = sums[turn(me, k), pl.ds(0, MAIN), :]


def final_kernel(*refs):
    parts, me, out = refs[:RING], refs[RING], refs[RING + 1]
    gather_chunks(me, out, parts)


def corrected(current, earlier, inertia, source, emitted, taken):
    mismatch = inertia * (current - earlier) + 4.0 * emitted * fourth(current) - taken - source
    slope = inertia + 16.0 * emitted * (current * current * current)
    return jnp.where(inertia > 0.0, current - mismatch / slope, 0.0)


def call(kernel, outs, scratch=(), space=pltpu.VMEM, smem=()):
    def run(*args):
        specs = [pl.BlockSpec(memory_space=pltpu.SMEM if n in smem else space) for n in range(len(args))]
        return pl.pallas_call(
            kernel,
            out_shape=[jax.ShapeDtypeStruct(dims, F32) for dims in outs],
            in_specs=specs,
            out_specs=[pl.BlockSpec(memory_space=pltpu.VMEM)] * len(outs),
            scratch_shapes=[pltpu.VMEM(s, F32) if isinstance(s, tuple) else s for s in scratch],
            compiler_params=pltpu.CompilerParams(vmem_limit_bytes=VMEM_LIMIT),
        )(*args)

    return run


FIELD = (4, 2, ROWS, TILE)
PADDED = (4, 2, ROWS + 2 * PAD, TILE)
SHARED = (2, 2, ROWS, TILE)
TURNS = (0, 1, 3, 2)


def along_y(array, by):
    pairs = [(4 * z + y, 4 * z + (y + by) % 4) for z in range(4) for y in range(4)]
    return lax.ppermute(array, "gas", pairs)


def sum_over_gas(parts):
    total = parts[0]
    for k in TURNS[1:]:
        total = total + along_y(parts[k], k)
    total = total + lax.ppermute(total, "gas", [(4 * z + y, 4 * (z ^ 1) + y) for z in range(4) for y in range(4)])
    return total + lax.ppermute(total, "gas", [(4 * z + y, 4 * (z ^ 2) + y) for z in range(4) for y in range(4)])


def spread(chunk):
    parts = {k: along_y(chunk, k) for k in TURNS[1:]}
    return [chunk] + [parts[k] for k in range(1, RING)]


def on_device(*inputs):
    kelvin, inertia, source, extinction, fractions, irradiance = inputs
    own = (extinction, fractions, irradiance, kelvin, inertia, source)
    own = [pltpu.with_memory_space_constraint(array, pltpu.HBM) for array in own]
    devices = lax.axis_size("space")
    across = 4
    me = lax.rem(lax.axis_index("gas"), RING).reshape(1)
    planes, up, down = call(
        load_kernel,
        [(PLANES, TILE, TILE)] + [(PLANES, HALO, TILE)] * 2,
        [pltpu.SemaphoreType.DMA((27,))],
        space=pltpu.HBM,
    )(*own)
    top = lax.ppermute(up, "space", [(i, i + across) for i in range(devices - across)])
    bottom = lax.ppermute(down, "space", [(i + across, i) for i in range(devices - across)])
    right, left = call(pack_y_kernel, [(PACKS, ROWS, TILE)] * 2)(planes, top, bottom)
    pairs = [(i, i + 1) for i in range(devices) if i % across != across - 1]
    from_left = lax.ppermute(right, "space", pairs)
    from_right = lax.ppermute(left, "space", [(j, i) for i, j in pairs])
    two = (2 * CHUNK, TILE)
    a, q, kap, now, held, *parts = call(
        first_kernel,
        [(5,) + FIELD, FIELD, PADDED, PADDED, (3, CHUNK, TILE)] + [two] * RING,
        [(6, 2, ROWS, TILE), FIELD, SHARED, PADDED, PADDED, (RING,) + two],
        smem=(5,),
    )(planes, top, bottom, from_left, from_right, me)
    total = sum_over_gas(parts)
    taken, emitted = total[:CHUNK], total[CHUNK:]
    earlier, inertia, source = held[0], held[1], held[2]
    current = corrected(earlier, earlier, inertia, source, emitted, taken)
    one = (CHUNK, TILE)
    now, *parts = call(
        next_kernel, [PADDED] + [one] * RING, [FIELD, SHARED, PADDED, (RING,) + one], smem=(8,)
    )(a, q, kap, now, *spread(current), me)
    current = corrected(current, earlier, inertia, source, emitted, sum_over_gas(parts))
    radiation, *parts = call(
        last_kernel,
        [(2, 1, 2, TILE, TILE)] + [(MAIN, TILE)] * RING,
        [FIELD, SHARED, PADDED, PADDED, (RING,) + one],
        smem=(8,),
    )(a, q, kap, now, *spread(current), me)
    rest = (value[:MAIN] for value in (current, earlier, inertia, source, emitted))
    current = corrected(*rest, sum_over_gas(parts))
    (final,) = call(final_kernel, [(RING, MAIN, TILE)], smem=(RING,))(*spread(current), me)
    return final.reshape(1, 2, TILE, TILE), radiation


def solution(mesh):
    placed = (
        P("space", None, None, None),
        P("space", None, None, None),
        P("space", None, None, None),
        P("gas", "space", None, None, None),
        P("gas", "space", None, None, None),
        P("gas", "space", None, None, None),
    )
    return jax.shard_map(
        on_device,
        mesh=mesh,
        in_specs=placed,
        out_specs=(P("space", None, None, None), P("gas", "space", None, None, None)),
        check_vma=False,
    )
```

```python
import functools

import jax
import jax.numpy as jnp
from jax import lax
from jax.experimental import pallas as pl
from jax.experimental.pallas import tpu as pltpu
from jax.sharding import PartitionSpec as P

SWEEPS = 8
OUTER = 3
LOW_BOUND = 0.05
HIGH_BOUND = 2.0

TILE = 128
HALO = SWEEPS * OUTER
ROWS = TILE + 2 * HALO
PAD = 8
STEP = 16
PLANES = 16
PACKS = 3
ACROSS = 4
RING = 4
MAIN = 64
FULL = 80
CHUNK = 104
SIDE = 16
VMEM_LIMIT = 16 * 1024 * 1024
F32 = jnp.float32


def sweep_weights():
    theta_mid = (HIGH_BOUND + LOW_BOUND) / 2.0
    delta_half = (HIGH_BOUND - LOW_BOUND) / 2.0
    sigma_ratio = theta_mid / delta_half
    rho_now = 1.0 / sigma_ratio
    weights = [(0.0, 1.0 / theta_mid)]
    for _ in range(SWEEPS - 1):
        rho_next = 1.0 / (2.0 * sigma_ratio - rho_now)
        weights.append((rho_next * rho_now, 2.0 * rho_next / delta_half))
        rho_now = rho_next
    return weights


def place_in_space():
    place = lax.axis_index("space")
    return place >> 2, place & 3


def owner():
    return lax.axis_index("gas") & 3


def load_kernel(*refs):
    planes, up, down, sems = refs[6:]
    copies = []
    sources = [(refs[f].at[gas, 0], 4 * f + 2 * gas, 2) for f in range(3) for gas in range(2)]
    sources.append((refs[3].at[0], 12, 2))
    layer = owner() >> 1
    sources += [(refs[4 + f].at[0, pl.ds(layer, 1)], 14 + f, 1) for f in range(2)]
    for source, first, layers in sources:
        for row, count, out in ((TILE - HALO, HALO, up), (0, HALO, down), (0, TILE, planes)):
            copies.append(
                pltpu.make_async_copy(
                    source.at[:, pl.ds(row, count), :], out.at[pl.ds(first, layers)], sems.at[len(copies)]
                )
            )
    for copy in copies:
        copy.start()
    for copy in copies:
        copy.wait()


def slot(p):
    pack, lane = divmod(HALO * p, TILE)
    return pack, lane, [pack] if lane + HALO <= TILE else [pack, pack + 1]


def pack_y_kernel(planes, top, bottom, first, second):
    tile_row, column = place_in_space()
    odd = (column & 1) == 1
    for row in range(0, ROWS, 8):
        lane = lax.broadcasted_iota(jnp.int32, (8, TILE), 1)
        to_right = [jnp.zeros((8, TILE), F32) for _ in range(PACKS)]
        to_left = [jnp.zeros((8, TILE), F32) for _ in range(PACKS)]
        for p in range(PLANES):
            if row < HALO:
                value = jnp.where(tile_row > 0, top[p, pl.ds(row, 8), :], 0.0)
            elif row < HALO + TILE:
                value = planes[p, pl.ds(row - HALO, 8), :]
            else:
                value = jnp.where(tile_row < ACROSS - 1, bottom[p, pl.ds(row - HALO - TILE, 8), :], 0.0)
            _, start, packs = slot(p)
            left = pltpu.roll(value, start, 1) if start else value
            right = pltpu.roll(value, (start + HALO) % TILE, 1)
            for pack in packs:
                at = lane + TILE * pack
                here = (at >= HALO * p) & (at < HALO * (p + 1))
                to_left[pack] = jnp.where(here, left, to_left[pack])
                to_right[pack] = jnp.where(here, right, to_right[pack])
        for pack in range(PACKS):
            first[pack, pl.ds(row, 8), :] = jnp.where(odd, to_left[pack], to_right[pack])
            second[pack, pl.ds(row, 8), :] = jnp.where(odd, to_right[pack], to_left[pack])


def chunk_rows(half):
    return [HALO + MAIN * half + 8 * k for k in range(8)] + ([8, 16], [ROWS - 24, ROWS - 16])[half]


def chunk_out(out, field, first=0):
    lane = lax.broadcasted_iota(jnp.int32, (8, TILE), 1)
    for c in range(RING):
        z, rows = c // 2, chunk_rows(c % 2)
        for k, row in enumerate(rows):
            out[c, pl.ds(first + 8 * k, 8), :] = field[z, 0, pl.ds(row, 8), :]
        for slot in range(3):
            packed = jnp.zeros((8, TILE), F32)
            for j, k in enumerate(range(slot, 10, 3)):
                value = pltpu.roll(field[z, 1, pl.ds(rows[k], 8), :], (SIDE + 32 * j) % TILE, 1)
                packed = jnp.where((lane >= 32 * j) & (lane < 32 * (j + 1)), value, packed)
            out[c, pl.ds(first + FULL + 8 * slot, 8), :] = packed


def chunk_in(field, chunks, change):
    for c in range(RING):
        z, rows = c // 2, chunk_rows(c % 2)
        for k, row in enumerate(rows):
            field[z, 0, pl.ds(row, 8), :] = change(chunks[c, pl.ds(8 * k, 8), :])
            packed = change(chunks[c, pl.ds(FULL + 8 * (k % 3), 8), :])
            field[z, 1, pl.ds(row, 8), :] = pltpu.roll(packed, (TILE - SIDE - 32 * (k // 3)) % TILE, 1)


def own_chunk(out, layer):
    lane = lax.broadcasted_iota(jnp.int32, (8, TILE), 1)
    half = owner() & 1
    low, high = chunk_rows(0), chunk_rows(1)
    rows = [pl.multiple_of(a + (b - a) * half, 8) for a, b in zip(low, high)]
    for k, row in enumerate(rows):
        out[pl.ds(8 * k, 8), :] = layer[0, pl.ds(row, 8), :]
    for slot_of in range(3):
        packed = jnp.zeros((8, TILE), F32)
        for j, k in enumerate(range(slot_of, 10, 3)):
            value = pltpu.roll(layer[1, pl.ds(rows[k], 8), :], (SIDE + 32 * j) % TILE, 1)
            packed = jnp.where((lane >= 32 * j) & (lane < 32 * (j + 1)), value, packed)
        out[pl.ds(FULL + 8 * slot_of, 8), :] = packed


def turn(k):
    return (owner() + k) & 3


def send_chunks(chunks, outs):
    for k, out in enumerate(outs):
        out[...] = chunks[turn(k)]


def gather_chunks(chunks, parts):
    for k, part in enumerate(parts):
        chunks[turn(RING - k)] = part[...]


def fourth(value):
    square = value * value
    return square * square


def left_right(own, other, lane):
    left = pltpu.roll(jnp.where(lane == TILE - 1, other, own), 1, 1)
    right = pltpu.roll(jnp.where(lane == 0, other, own), TILE - 1, 1)
    return left, right


def each_step(first, last, body):
    for r in range(first, last, STEP):
        body(r)


def solve(step, a, q, t4, sp, start, now, old):
    first, last = 8 * step, ROWS - 8 * step

    def source(r):
        for gz in range(4):
            for l in range(2):
                weight = q[gz, l, pl.ds(r, STEP), :]
                value = weight * t4[gz % 2, l, pl.ds(r, STEP), :]
                sp[gz, l, pl.ds(r, STEP), :] = jnp.where(weight > 0.0, value, 0.0)

    each_step(first, last, source)
    before, src = None, start
    for sweep, (keep, push) in enumerate(sweep_weights()):
        dst = old if sweep % 2 == 0 else now

        def body(r, src=src, dst=dst, before=before, keep=keep, push=push):
            lane = lax.broadcasted_iota(jnp.int32, (STEP, TILE), 1)
            rows = pl.ds(r, STEP)
            for g in range(2):
                own = [[src[2 * g + z, l, pl.ds(r + PAD, STEP), :] for l in range(2)] for z in range(2)]
                for z in range(2):
                    for l in range(2):
                        gz = 2 * g + z
                        here = own[z][l]
                        left, right = left_right(here, own[z][1 - l], lane)
                        total = sp[gz, l, rows, :] + a[0, gz, l, rows, :] * own[1 - z][l]
                        total += a[1, gz, l, rows, :] * src[gz, l, pl.ds(r + PAD - 1, STEP), :]
                        total += a[2, gz, l, rows, :] * src[gz, l, pl.ds(r + PAD + 1, STEP), :]
                        total += a[3, gz, l, rows, :] * left + a[4, gz, l, rows, :] * right
                        value = (1.0 + keep - push) * here + push * total
                        if before is not None:
                            value -= keep * before[gz, l, pl.ds(r + PAD, STEP), :]
                        dst[gz, l, pl.ds(r + PAD, STEP), :] = value

        each_step(first, last, body)
        before, src = src, dst


def absorb(kap, now, out):
    def body(r):
        for z in range(2):
            for l in range(2):
                rows = pl.ds(r + PAD, STEP)
                out[z, l, pl.ds(r, STEP), :] = (
                    kap[z, l, rows, :] * now[z, l, rows, :] + kap[2 + z, l, rows, :] * now[2 + z, l, rows, :]
                )

    each_step(8, ROWS - 8, body)


def first_kernel(planes, top, bottom, first, second, *refs):
    a, q, kap, now, held, *outs = refs[: 5 + RING]
    tis, sp, t4, old, begin, sums = refs[5 + RING :]
    planck = now
    tile_row, column = place_in_space()
    odd = (column & 1) == 1

    def place(p):
        if p < 4:
            return kap, p, PAD
        if p < 8:
            return q, p - 4, 0
        if p < 12:
            return begin, p - 8, PAD
        return tis, p - 12, 0

    for p in range(PLANES):
        dst, at, pad = place(p)
        dst[at, 0, pl.ds(pad, HALO), :] = jnp.where(tile_row > 0, top[p], 0.0)
        dst[at, 0, pl.ds(pad + HALO, TILE), :] = planes[p]
        dst[at, 0, pl.ds(pad + HALO + TILE, HALO), :] = jnp.where(tile_row < ACROSS - 1, bottom[p], 0.0)

    def sides(r):
        lane = lax.broadcasted_iota(jnp.int32, (STEP, TILE), 1)
        got = [(first[pack, pl.ds(r, STEP), :], second[pack, pl.ds(r, STEP), :]) for pack in range(PACKS)]
        lefts = [jnp.where(column > 0, jnp.where(odd, f, s), 0.0) for f, s in got]
        rights = [jnp.where(column < ACROSS - 1, jnp.where(odd, s, f), 0.0) for f, s in got]
        for p in range(PLANES):
            pack, start, packs = slot(p)
            left, right = lefts[pack], rights[pack]
            if len(packs) > 1:
                left = jnp.where(lane >= start, left, lefts[pack + 1])
                right = jnp.where(lane >= start, right, rights[pack + 1])
            left = pltpu.roll(left, (2 * TILE - HALO - start) % TILE, 1)
            right = pltpu.roll(right, TILE - start, 1) if start else right
            dst, at, pad = place(p)
            value = jnp.where(lane < HALO, right, jnp.where(lane >= TILE - HALO, left, 0.0))
            dst[at, 1, pl.ds(r + pad, STEP), :] = value

    each_step(0, ROWS, sides)
    own_chunk(held.at[0], tis.at[owner() >> 1])
    own_chunk(held.at[1], tis.at[2])
    own_chunk(held.at[2], tis.at[3])

    def halves(r):
        lane = lax.broadcasted_iota(jnp.int32, (STEP, TILE), 1)
        rows, padded = pl.ds(r, STEP), pl.ds(r + PAD, STEP)
        for z in range(2):
            for l in range(2):
                t4[z, l, rows, :] = fourth(tis[z, l, rows, :])
                planck[z, l, rows, :] = (
                    kap[z, l, padded, :] * q[z, l, rows, :] + kap[2 + z, l, padded, :] * q[2 + z, l, rows, :]
                )
        for gz in range(4):
            own = [kap[gz, l, padded, :] for l in range(2)]
            for l in range(2):
                old[gz, l, padded, :] = 1.0 / (own[l] + kap[gz, l, pl.ds(r + PAD + 1, STEP), :])
                sp[gz, l, rows, :] = 1.0 / (own[l] + left_right(own[l], own[1 - l], lane)[1])

    each_step(0, ROWS, halves)

    def coefficients(r):
        lane = lax.broadcasted_iota(jnp.int32, (STEP, TILE), 1)
        rows, padded = pl.ds(r, STEP), pl.ds(r + PAD, STEP)
        for g in range(2):
            own = [[kap[2 * g + z, l, padded, :] for l in range(2)] for z in range(2)]
            between = [1.0 / (own[0][l] + own[1][l]) for l in range(2)]
            for z in range(2):
                gz = 2 * g + z
                to_right = [sp[gz, l, rows, :] for l in range(2)]
                for l in range(2):
                    here = own[z][l]
                    to_left = left_right(to_right[l], to_right[1 - l], lane)[0]
                    to_up = old[gz, l, pl.ds(r + PAD - 1, STEP), :]
                    couplings = [between[l], to_up, old[gz, l, padded, :], to_left, to_right[l]]
                    diagonal = 1.5 * here + 1.0 / here
                    for coupling in couplings:
                        diagonal += coupling
                    inverse = 1.0 / diagonal
                    for f, coupling in enumerate(couplings):
                        a[f, gz, l, rows, :] = jnp.where(here > 0.0, coupling * inverse, 0.0)
                    weight = 6.0 * here * q[gz, l, rows, :] * inverse
                    q[gz, l, rows, :] = jnp.where(here > 0.0, weight, 0.0)

    each_step(0, ROWS, coefficients)
    chunk_out(sums, planck, CHUNK)
    solve(0, a, q, t4, sp, begin, now, old)
    absorb(kap, now, t4)
    chunk_out(sums, t4)
    send_chunks(sums, outs)


def next_kernel(a, q, kap, start, *refs):
    parts = refs[:RING]
    now, *outs = refs[RING : 2 * RING + 1]
    sp, t4, old, sums = refs[2 * RING + 1 :]
    gather_chunks(sums, parts)
    chunk_in(t4, sums, fourth)
    solve(1, a, q, t4, sp, start, now, old)
    absorb(kap, now, t4)
    chunk_out(sums, t4)
    send_chunks(sums, outs)


def last_kernel(a, q, kap, start, *refs):
    parts = refs[:RING]
    radiation, *outs = refs[RING : 2 * RING + 1]
    sp, t4, old, now, sums = refs[2 * RING + 1 :]
    gather_chunks(sums, parts)
    chunk_in(t4, sums, fourth)
    solve(2, a, q, t4, sp, start, now, old)
    rows = pl.ds(PAD + HALO, TILE)
    for gz in range(4):
        radiation[gz // 2, 0, gz % 2, :, :] = now[gz, 0, rows, :]
    for c in range(RING):
        z = c // 2
        part = pl.ds(PAD + HALO + MAIN * (c % 2), MAIN)
        sums[c, pl.ds(0, MAIN), :] = (
            kap[z, 0, part, :] * now[z, 0, part, :] + kap[2 + z, 0, part, :] * now[2 + z, 0, part, :]
        )
    for k, out in enumerate(outs):
        out[...] = sums[turn(k), pl.ds(0, MAIN), :]


def final_kernel(*refs):
    parts, out = refs[:RING], refs[RING]
    gather_chunks(out, parts)


def corrected(current, earlier, inertia, source, emitted, taken):
    mismatch = inertia * (current - earlier) + 4.0 * emitted * fourth(current) - taken - source
    slope = inertia + 16.0 * emitted * (current * current * current)
    return jnp.where(inertia > 0.0, current - mismatch / slope, 0.0)


def call(kernel, outs, scratch=(), space=pltpu.VMEM):
    def run(*args):
        return pl.pallas_call(
            kernel,
            out_shape=[jax.ShapeDtypeStruct(dims, F32) for dims in outs],
            in_specs=[pl.BlockSpec(memory_space=space)] * len(args),
            out_specs=[pl.BlockSpec(memory_space=pltpu.VMEM)] * len(outs),
            scratch_shapes=[pltpu.VMEM(s, F32) if isinstance(s, tuple) else s for s in scratch],
            compiler_params=pltpu.CompilerParams(vmem_limit_bytes=VMEM_LIMIT),
        )(*args)

    return run


FIELD = (4, 2, ROWS, TILE)
PADDED = (4, 2, ROWS + 2 * PAD, TILE)
SHARED = (2, 2, ROWS, TILE)
OUT_TURNS = (2, 1, 3)
BACK_TURNS = (1, 3, 2)


def along_y(array, by):
    pairs = [(4 * z + y, 4 * z + (y + by) % 4) for z in range(4) for y in range(4)]
    return lax.ppermute(array, "gas", pairs)


def along_z(array, by):
    pairs = [(4 * z + y, 4 * ((z + by) % 4) + y) for z in range(4) for y in range(4)]
    return lax.ppermute(array, "gas", pairs)


def sum_over_gas(parts):
    total = parts[0]
    for k in OUT_TURNS:
        total = total + along_y(parts[k], k)
    parts = [along_z(total, k) for k in (2, 1, 3)]
    return total + parts[0] + parts[1] + parts[2]


def spread(chunk):
    parts = {k: along_y(chunk, k) for k in BACK_TURNS}
    return [chunk] + [parts[k] for k in range(1, RING)]


def on_device(*inputs):
    kelvin, inertia, source, extinction, fractions, irradiance = inputs
    own = (extinction, fractions, irradiance, kelvin, inertia, source)
    own = [pltpu.with_memory_space_constraint(array, pltpu.HBM) for array in own]
    devices = lax.axis_size("space")
    planes, up, down = call(
        load_kernel,
        [(PLANES, TILE, TILE)] + [(PLANES, HALO, TILE)] * 2,
        [pltpu.SemaphoreType.DMA((27,))],
        space=pltpu.HBM,
    )(*own)
    ring = [(i, (i + ACROSS) % devices) for i in range(devices)]
    top = lax.ppermute(up, "space", ring)
    bottom = lax.ppermute(down, "space", [(j, i) for i, j in ring])
    first, second = call(pack_y_kernel, [(PACKS, ROWS, TILE)] * 2)(planes, top, bottom)
    first = lax.ppermute(first, "space", [(i, i ^ 1) for i in range(devices)])
    swaps = (0, 2, 1, 3)
    second = lax.ppermute(second, "space", [(i, i - i % ACROSS + swaps[i % ACROSS]) for i in range(devices)])
    two = (2 * CHUNK, TILE)
    a, q, kap, now, held, *parts = call(
        first_kernel,
        [(5,) + FIELD, FIELD, PADDED, PADDED, (3, CHUNK, TILE)] + [two] * RING,
        [(4, 2, ROWS, TILE), FIELD, SHARED, PADDED, PADDED, (RING,) + two],
    )(planes, top, bottom, first, second)
    total = sum_over_gas(parts)
    taken, emitted = total[:CHUNK], total[CHUNK:]
    earlier, inertia, source = held[0], held[1], held[2]
    current = corrected(earlier, earlier, inertia, source, emitted, taken)
    one = (CHUNK, TILE)
    now, *parts = call(
        next_kernel, [PADDED] + [one] * RING, [FIELD, SHARED, PADDED, (RING,) + one]
    )(a, q, kap, now, *spread(current))
    current = corrected(current, earlier, inertia, source, emitted, sum_over_gas(parts))
    radiation, *parts = call(
        last_kernel,
        [(2, 1, 2, TILE, TILE)] + [(MAIN, TILE)] * RING,
        [FIELD, SHARED, PADDED, PADDED, (RING,) + one],
    )(a, q, kap, now, *spread(current))
    rest = (value[:MAIN] for value in (current, earlier, inertia, source, emitted))
    current = corrected(*rest, sum_over_gas(parts))
    (final,) = call(final_kernel, [(RING, MAIN, TILE)])(*spread(current))
    return final.reshape(1, 2, TILE, TILE), radiation


def solution(mesh):
    placed = (
        P("space", None, None, None),
        P("space", None, None, None),
        P("space", None, None, None),
        P("gas", "space", None, None, None),
        P("gas", "space", None, None, None),
        P("gas", "space", None, None, None),
    )
    return jax.shard_map(
        on_device,
        mesh=mesh,
        in_specs=placed,
        out_specs=(P("space", None, None, None), P("gas", "space", None, None, None)),
        check_vma=False,
    )
```

```python
import functools

import jax
import jax.numpy as jnp
from jax import lax
from jax.experimental import pallas as pl
from jax.experimental.pallas import tpu as pltpu
from jax.sharding import PartitionSpec as P

SWEEPS = 8
OUTER = 3
LOW_BOUND = 0.05
HIGH_BOUND = 2.0

TILE = 128
HALO = SWEEPS * OUTER
ROWS = TILE + 2 * HALO
PAD = 8
STEP = 16
PLANES = 16
PACKS = 3
ACROSS = 4
RING = 4
MAIN = 64
FULL = 80
CHUNK = 104
SIDE = 16
VMEM_LIMIT = 16 * 1024 * 1024
F32 = jnp.float32


def sweep_weights():
    theta_mid = (HIGH_BOUND + LOW_BOUND) / 2.0
    delta_half = (HIGH_BOUND - LOW_BOUND) / 2.0
    sigma_ratio = theta_mid / delta_half
    rho_now = 1.0 / sigma_ratio
    weights = [(0.0, 1.0 / theta_mid)]
    for _ in range(SWEEPS - 1):
        rho_next = 1.0 / (2.0 * sigma_ratio - rho_now)
        weights.append((rho_next * rho_now, 2.0 * rho_next / delta_half))
        rho_now = rho_next
    return weights


def load_kernel(*refs):
    me, planes, up, down, sems = refs[6:]
    copies = []
    sources = [(refs[f].at[gas, 0], 4 * f + 2 * gas, 2) for f in range(3) for gas in range(2)]
    sources.append((refs[3].at[0], 12, 2))
    layer = me[0] >> 1
    sources += [(refs[4 + f].at[0, pl.ds(layer, 1)], 14 + f, 1) for f in range(2)]
    for source, first, layers in sources:
        for row, count, out in ((TILE - HALO, HALO, up), (0, HALO, down), (0, TILE, planes)):
            copies.append(
                pltpu.make_async_copy(
                    source.at[:, pl.ds(row, count), :], out.at[pl.ds(first, layers)], sems.at[len(copies)]
                )
            )
    for copy in copies:
        copy.start()
    for copy in copies:
        copy.wait()


def slot(p):
    pack, lane = divmod(HALO * p, TILE)
    return pack, lane, [pack] if lane + HALO <= TILE else [pack, pack + 1]


def pack_y_kernel(planes, top, bottom, tile_row_ref, column_ref, first, second):
    tile_row, column = tile_row_ref[0], column_ref[0]
    odd = (column & 1) == 1
    for row in range(0, ROWS, 8):
        lane = lax.broadcasted_iota(jnp.int32, (8, TILE), 1)
        to_right = [jnp.zeros((8, TILE), F32) for _ in range(PACKS)]
        to_left = [jnp.zeros((8, TILE), F32) for _ in range(PACKS)]
        for p in range(PLANES):
            if row < HALO:
                value = jnp.where(tile_row > 0, top[p, pl.ds(row, 8), :], 0.0)
            elif row < HALO + TILE:
                value = planes[p, pl.ds(row - HALO, 8), :]
            else:
                value = jnp.where(tile_row < ACROSS - 1, bottom[p, pl.ds(row - HALO - TILE, 8), :], 0.0)
            _, start, packs = slot(p)
            left = pltpu.roll(value, start, 1) if start else value
            right = pltpu.roll(value, (start + HALO) % TILE, 1)
            for pack in packs:
                at = lane + TILE * pack
                here = (at >= HALO * p) & (at < HALO * (p + 1))
                to_left[pack] = jnp.where(here, left, to_left[pack])
                to_right[pack] = jnp.where(here, right, to_right[pack])
        for pack in range(PACKS):
            first[pack, pl.ds(row, 8), :] = jnp.where(odd, to_left[pack], to_right[pack])
            second[pack, pl.ds(row, 8), :] = jnp.where(odd, to_right[pack], to_left[pack])


def chunk_rows(half):
    return [HALO + MAIN * half + 8 * k for k in range(8)] + ([8, 16], [ROWS - 24, ROWS - 16])[half]


def chunk_out(out, field, first=0):
    lane = lax.broadcasted_iota(jnp.int32, (8, TILE), 1)
    for c in range(RING):
        z, rows = c // 2, chunk_rows(c % 2)
        for k, row in enumerate(rows):
            out[c, pl.ds(first + 8 * k, 8), :] = field[z, 0, pl.ds(row, 8), :]
        for slot in range(3):
            packed = jnp.zeros((8, TILE), F32)
            for j, k in enumerate(range(slot, 10, 3)):
                value = pltpu.roll(field[z, 1, pl.ds(rows[k], 8), :], (SIDE + 32 * j) % TILE, 1)
                packed = jnp.where((lane >= 32 * j) & (lane < 32 * (j + 1)), value, packed)
            out[c, pl.ds(first + FULL + 8 * slot, 8), :] = packed


def chunk_in(field, chunks, change):
    for c in range(RING):
        z, rows = c // 2, chunk_rows(c % 2)
        for k, row in enumerate(rows):
            field[z, 0, pl.ds(row, 8), :] = change(chunks[c, pl.ds(8 * k, 8), :])
            packed = change(chunks[c, pl.ds(FULL + 8 * (k % 3), 8), :])
            field[z, 1, pl.ds(row, 8), :] = pltpu.roll(packed, (TILE - SIDE - 32 * (k // 3)) % TILE, 1)


def own_chunk(me, out, layer):
    lane = lax.broadcasted_iota(jnp.int32, (8, TILE), 1)
    half = me[0] & 1
    low, high = chunk_rows(0), chunk_rows(1)
    rows = [pl.multiple_of(a + (b - a) * half, 8) for a, b in zip(low, high)]
    for k, row in enumerate(rows):
        out[pl.ds(8 * k, 8), :] = layer[0, pl.ds(row, 8), :]
    for slot_of in range(3):
        packed = jnp.zeros((8, TILE), F32)
        for j, k in enumerate(range(slot_of, 10, 3)):
            value = pltpu.roll(layer[1, pl.ds(rows[k], 8), :], (SIDE + 32 * j) % TILE, 1)
            packed = jnp.where((lane >= 32 * j) & (lane < 32 * (j + 1)), value, packed)
        out[pl.ds(FULL + 8 * slot_of, 8), :] = packed


def turn(me, k):
    return (me[0] + k) & 3


def send_chunks(me, chunks, outs):
    for k, out in enumerate(outs):
        out[...] = chunks[turn(me, k)]


def gather_chunks(me, chunks, parts):
    for k, part in zip(BACK, parts):
        chunks[turn(me, RING - k)] = part[...]


def fourth(value):
    square = value * value
    return square * square


def left_right(own, other, lane):
    left = pltpu.roll(jnp.where(lane == TILE - 1, other, own), 1, 1)
    right = pltpu.roll(jnp.where(lane == 0, other, own), TILE - 1, 1)
    return left, right


def each_step(first, last, body):
    for r in range(first, last, STEP):
        body(r)


def solve(step, a, q, t4, sp, start, now, old):
    first, last = 8 * step, ROWS - 8 * step

    def source(r):
        for gz in range(4):
            for l in range(2):
                weight = q[gz, l, pl.ds(r, STEP), :]
                value = weight * t4[gz % 2, l, pl.ds(r, STEP), :]
                sp[gz, l, pl.ds(r, STEP), :] = jnp.where(weight > 0.0, value, 0.0)

    each_step(first, last, source)
    before, src = None, start
    for sweep, (keep, push) in enumerate(sweep_weights()):
        dst = old if sweep % 2 == 0 else now

        def body(r, src=src, dst=dst, before=before, keep=keep, push=push):
            lane = lax.broadcasted_iota(jnp.int32, (STEP, TILE), 1)
            rows = pl.ds(r, STEP)
            for g in range(2):
                own = [[src[2 * g + z, l, pl.ds(r + PAD, STEP), :] for l in range(2)] for z in range(2)]
                for z in range(2):
                    for l in range(2):
                        gz = 2 * g + z
                        here = own[z][l]
                        left, right = left_right(here, own[z][1 - l], lane)
                        total = sp[gz, l, rows, :] + a[0, gz, l, rows, :] * own[1 - z][l]
                        total += a[1, gz, l, rows, :] * src[gz, l, pl.ds(r + PAD - 1, STEP), :]
                        total += a[2, gz, l, rows, :] * src[gz, l, pl.ds(r + PAD + 1, STEP), :]
                        total += a[3, gz, l, rows, :] * left + a[4, gz, l, rows, :] * right
                        value = (1.0 + keep - push) * here + push * total
                        if before is not None:
                            value -= keep * before[gz, l, pl.ds(r + PAD, STEP), :]
                        dst[gz, l, pl.ds(r + PAD, STEP), :] = value

        each_step(first, last, body)
        before, src = src, dst


def absorb(kap, now, out):
    def body(r):
        for z in range(2):
            for l in range(2):
                rows = pl.ds(r + PAD, STEP)
                out[z, l, pl.ds(r, STEP), :] = (
                    kap[z, l, rows, :] * now[z, l, rows, :] + kap[2 + z, l, rows, :] * now[2 + z, l, rows, :]
                )

    each_step(8, ROWS - 8, body)


def first_kernel(planes, top, bottom, first, second, me, tile_row_ref, column_ref, *refs):
    a, q, kap, now, held, *outs = refs[: 5 + RING]
    tis, sp, t4, old, begin, sums = refs[5 + RING :]
    planck = now
    tile_row, column = tile_row_ref[0], column_ref[0]
    odd = (column & 1) == 1

    def place(p):
        if p < 4:
            return kap, p, PAD
        if p < 8:
            return q, p - 4, 0
        if p < 12:
            return begin, p - 8, PAD
        return tis, p - 12, 0

    for p in range(PLANES):
        dst, at, pad = place(p)
        dst[at, 0, pl.ds(pad, HALO), :] = jnp.where(tile_row > 0, top[p], 0.0)
        dst[at, 0, pl.ds(pad + HALO, TILE), :] = planes[p]
        dst[at, 0, pl.ds(pad + HALO + TILE, HALO), :] = jnp.where(tile_row < ACROSS - 1, bottom[p], 0.0)

    def sides(r):
        lane = lax.broadcasted_iota(jnp.int32, (STEP, TILE), 1)
        got = [(first[pack, pl.ds(r, STEP), :], second[pack, pl.ds(r, STEP), :]) for pack in range(PACKS)]
        lefts = [jnp.where(column > 0, jnp.where(odd, f, s), 0.0) for f, s in got]
        rights = [jnp.where(column < ACROSS - 1, jnp.where(odd, s, f), 0.0) for f, s in got]
        for p in range(PLANES):
            pack, start, packs = slot(p)
            left, right = lefts[pack], rights[pack]
            if len(packs) > 1:
                left = jnp.where(lane >= start, left, lefts[pack + 1])
                right = jnp.where(lane >= start, right, rights[pack + 1])
            left = pltpu.roll(left, (2 * TILE - HALO - start) % TILE, 1)
            right = pltpu.roll(right, TILE - start, 1) if start else right
            dst, at, pad = place(p)
            value = jnp.where(lane < HALO, right, jnp.where(lane >= TILE - HALO, left, 0.0))
            dst[at, 1, pl.ds(r + pad, STEP), :] = value

    each_step(0, ROWS, sides)
    own_chunk(me, held.at[0], tis.at[me[0] >> 1])
    own_chunk(me, held.at[1], tis.at[2])
    own_chunk(me, held.at[2], tis.at[3])

    def halves(r):
        lane = lax.broadcasted_iota(jnp.int32, (STEP, TILE), 1)
        rows, padded = pl.ds(r, STEP), pl.ds(r + PAD, STEP)
        for z in range(2):
            for l in range(2):
                t4[z, l, rows, :] = fourth(tis[z, l, rows, :])
                planck[z, l, rows, :] = (
                    kap[z, l, padded, :] * q[z, l, rows, :] + kap[2 + z, l, padded, :] * q[2 + z, l, rows, :]
                )
        for gz in range(4):
            own = [kap[gz, l, padded, :] for l in range(2)]
            for l in range(2):
                old[gz, l, padded, :] = 1.0 / (own[l] + kap[gz, l, pl.ds(r + PAD + 1, STEP), :])
                sp[gz, l, rows, :] = 1.0 / (own[l] + left_right(own[l], own[1 - l], lane)[1])

    each_step(0, ROWS, halves)

    def coefficients(r):
        lane = lax.broadcasted_iota(jnp.int32, (STEP, TILE), 1)
        rows, padded = pl.ds(r, STEP), pl.ds(r + PAD, STEP)
        for g in range(2):
            own = [[kap[2 * g + z, l, padded, :] for l in range(2)] for z in range(2)]
            between = [1.0 / (own[0][l] + own[1][l]) for l in range(2)]
            for z in range(2):
                gz = 2 * g + z
                to_right = [sp[gz, l, rows, :] for l in range(2)]
                for l in range(2):
                    here = own[z][l]
                    to_left = left_right(to_right[l], to_right[1 - l], lane)[0]
                    to_up = old[gz, l, pl.ds(r + PAD - 1, STEP), :]
                    couplings = [between[l], to_up, old[gz, l, padded, :], to_left, to_right[l]]
                    diagonal = 1.5 * here + 1.0 / here
                    for coupling in couplings:
                        diagonal += coupling
                    inverse = 1.0 / diagonal
                    for f, coupling in enumerate(couplings):
                        a[f, gz, l, rows, :] = jnp.where(here > 0.0, coupling * inverse, 0.0)
                    weight = 6.0 * here * q[gz, l, rows, :] * inverse
                    q[gz, l, rows, :] = jnp.where(here > 0.0, weight, 0.0)

    each_step(0, ROWS, coefficients)
    chunk_out(sums, planck, CHUNK)
    solve(0, a, q, t4, sp, begin, now, old)
    absorb(kap, now, t4)
    chunk_out(sums, t4)
    send_chunks(me, sums, outs)


def next_kernel(a, q, kap, start, *refs):
    parts, me = refs[:RING], refs[RING]
    now, *outs = refs[RING + 1 : 2 * RING + 2]
    sp, t4, old, sums = refs[2 * RING + 2 :]
    gather_chunks(me, sums, parts)
    chunk_in(t4, sums, fourth)
    solve(1, a, q, t4, sp, start, now, old)
    absorb(kap, now, t4)
    chunk_out(sums, t4)
    send_chunks(me, sums, outs)


def last_kernel(a, q, kap, start, *refs):
    parts, me = refs[:RING], refs[RING]
    radiation, *outs = refs[RING + 1 : 2 * RING + 2]
    sp, t4, old, now, sums = refs[2 * RING + 2 :]
    gather_chunks(me, sums, parts)
    chunk_in(t4, sums, fourth)
    solve(2, a, q, t4, sp, start, now, old)
    rows = pl.ds(PAD + HALO, TILE)
    for gz in range(4):
        radiation[gz // 2, 0, gz % 2, :, :] = now[gz, 0, rows, :]
    for c in range(RING):
        z = c // 2
        part = pl.ds(PAD + HALO + MAIN * (c % 2), MAIN)
        sums[c, pl.ds(0, MAIN), :] = (
            kap[z, 0, part, :] * now[z, 0, part, :] + kap[2 + z, 0, part, :] * now[2 + z, 0, part, :]
        )
    for k, out in enumerate(outs):
        out[...] = sums[turn(me, k), pl.ds(0, MAIN), :]


def final_kernel(*refs):
    parts, me, out = refs[:RING], refs[RING], refs[RING + 1]
    gather_chunks(me, out, parts)


def corrected(current, earlier, inertia, source, emitted, taken):
    mismatch = inertia * (current - earlier) + 4.0 * emitted * fourth(current) - taken - source
    slope = inertia + 16.0 * emitted * (current * current * current)
    return jnp.where(inertia > 0.0, current - mismatch / slope, 0.0)


def call(kernel, outs, scratch=(), space=pltpu.VMEM):
    def run(*args):
        return pl.pallas_call(
            kernel,
            out_shape=[jax.ShapeDtypeStruct(dims, F32) for dims in outs],
            in_specs=[
                pl.BlockSpec(memory_space=pltpu.SMEM if array.dtype == jnp.int32 else space) for array in args
            ],
            out_specs=[pl.BlockSpec(memory_space=pltpu.VMEM)] * len(outs),
            scratch_shapes=[pltpu.VMEM(s, F32) if isinstance(s, tuple) else s for s in scratch],
            compiler_params=pltpu.CompilerParams(vmem_limit_bytes=VMEM_LIMIT),
        )(*args)

    return run


FIELD = (4, 2, ROWS, TILE)
PADDED = (4, 2, ROWS + 2 * PAD, TILE)
SHARED = (2, 2, ROWS, TILE)
OUT_TURNS = (2, 1, 3)
BACK = (0, 1, 3, 2)


def along_y(array, by):
    pairs = [(4 * z + y, 4 * z + (y + by) % 4) for z in range(4) for y in range(4)]
    return lax.ppermute(array, "gas", pairs)


def along_z(array, by):
    pairs = [(4 * z + y, 4 * ((z + by) % 4) + y) for z in range(4) for y in range(4)]
    return lax.ppermute(array, "gas", pairs)


def sum_over_gas(parts):
    total = parts[0]
    for k in OUT_TURNS:
        total = total + along_y(parts[k], k)
    parts = [along_z(total, k) for k in (3, 1, 2)]
    return total + parts[0] + parts[1] + parts[2]


def spread(chunk):
    return [along_y(chunk, k) if k else chunk for k in BACK]


def on_device(*inputs):
    kelvin, inertia, source, extinction, fractions, irradiance = inputs
    own = (extinction, fractions, irradiance, kelvin, inertia, source)
    own = [pltpu.with_memory_space_constraint(array, pltpu.HBM) for array in own]
    devices = lax.axis_size("space")
    me = (lax.axis_index("gas") & 3).reshape(1)
    place = lax.axis_index("space")
    at = ((place >> 2).reshape(1), (place & 3).reshape(1))
    planes, up, down = call(
        load_kernel,
        [(PLANES, TILE, TILE)] + [(PLANES, HALO, TILE)] * 2,
        [pltpu.SemaphoreType.DMA((27,))],
        space=pltpu.HBM,
    )(*own, me)
    ring = [(i, (i + ACROSS) % devices) for i in range(devices)]
    top = lax.ppermute(up, "space", ring)
    bottom = lax.ppermute(down, "space", [(j, i) for i, j in ring])
    first, second = call(pack_y_kernel, [(PACKS, ROWS, TILE)] * 2)(planes, top, bottom, *at)
    first = lax.ppermute(first, "space", [(i, i ^ 1) for i in range(devices)])
    swaps = (0, 2, 1, 3)
    second = lax.ppermute(second, "space", [(i, i - i % ACROSS + swaps[i % ACROSS]) for i in range(devices)])
    two = (2 * CHUNK, TILE)
    a, q, kap, now, held, *parts = call(
        first_kernel,
        [(5,) + FIELD, FIELD, PADDED, PADDED, (3, CHUNK, TILE)] + [two] * RING,
        [(4, 2, ROWS, TILE), FIELD, SHARED, PADDED, PADDED, (RING,) + two],
    )(planes, top, bottom, first, second, me, *at)
    total = sum_over_gas(parts)
    taken, emitted = total[:CHUNK], total[CHUNK:]
    earlier, inertia, source = held[0], held[1], held[2]
    current = corrected(earlier, earlier, inertia, source, emitted, taken)
    one = (CHUNK, TILE)
    now, *parts = call(
        next_kernel, [PADDED] + [one] * RING, [FIELD, SHARED, PADDED, (RING,) + one]
    )(a, q, kap, now, *spread(current), me)
    current = corrected(current, earlier, inertia, source, emitted, sum_over_gas(parts))
    radiation, *parts = call(
        last_kernel,
        [(2, 1, 2, TILE, TILE)] + [(MAIN, TILE)] * RING,
        [FIELD, SHARED, PADDED, PADDED, (RING,) + one],
    )(a, q, kap, now, *spread(current), me)
    rest = (value[:MAIN] for value in (current, earlier, inertia, source, emitted))
    current = corrected(*rest, sum_over_gas(parts))
    (final,) = call(final_kernel, [(RING, MAIN, TILE)])(*spread(current), me)
    return final.reshape(1, 2, TILE, TILE), radiation


def solution(mesh):
    placed = (
        P("space", None, None, None),
        P("space", None, None, None),
        P("space", None, None, None),
        P("gas", "space", None, None, None),
        P("gas", "space", None, None, None),
        P("gas", "space", None, None, None),
    )
    return jax.shard_map(
        on_device,
        mesh=mesh,
        in_specs=placed,
        out_specs=(P("space", None, None, None), P("gas", "space", None, None, None)),
        check_vma=False,
    )
```

```python
import functools

import jax
import jax.numpy as jnp
from jax import lax
from jax.experimental import pallas as pl
from jax.experimental.pallas import tpu as pltpu
from jax.sharding import PartitionSpec as P

SWEEPS = 8
OUTER = 3
LOW_BOUND = 0.05
HIGH_BOUND = 2.0

TILE = 128
HALO = SWEEPS * OUTER
ROWS = TILE + 2 * HALO
PAD = 8
STEP = 16
PLANES = 16
PACKS = 3
ACROSS = 4
RING = 4
MAIN = 64
FULL = 80
CHUNK = 104
SIDE = 16
VMEM_LIMIT = 16 * 1024 * 1024
F32 = jnp.float32


def sweep_weights():
    theta_mid = (HIGH_BOUND + LOW_BOUND) / 2.0
    delta_half = (HIGH_BOUND - LOW_BOUND) / 2.0
    sigma_ratio = theta_mid / delta_half
    rho_now = 1.0 / sigma_ratio
    weights = [(0.0, 1.0 / theta_mid)]
    for _ in range(SWEEPS - 1):
        rho_next = 1.0 / (2.0 * sigma_ratio - rho_now)
        weights.append((rho_next * rho_now, 2.0 * rho_next / delta_half))
        rho_now = rho_next
    return weights


def field_sources(refs, me):
    sources = [(refs[f].at[gas, 0], 4 * f + 2 * gas, 2) for f in range(3) for gas in range(2)]
    sources.append((refs[3].at[0], 12, 2))
    layer = me[0] >> 1
    return sources + [(refs[4 + f].at[0, pl.ds(layer, 1)], 14 + f, 1) for f in range(2)]


def copy_rows(refs, me, parts, sems):
    copies = []
    for source, first, layers in field_sources(refs, me):
        for row, count, out in parts:
            copies.append(
                pltpu.make_async_copy(
                    source.at[:, pl.ds(row, count), :], out.at[pl.ds(first, layers)], sems.at[len(copies)]
                )
            )
    for copy in copies:
        copy.start()
    for copy in copies:
        copy.wait()


def edge_kernel(*refs):
    me, up, down, sems = refs[6:]
    copy_rows(refs[:6], me, ((TILE - HALO, HALO, up), (0, HALO, down)), sems)


def load_kernel(*refs):
    me, planes, sems = refs[6:]
    copy_rows(refs[:6], me, ((0, TILE, planes),), sems)


def slot(p):
    pack, lane = divmod(HALO * p, TILE)
    return pack, lane, [pack] if lane + HALO <= TILE else [pack, pack + 1]


def pack_y_kernel(planes, top, bottom, tile_row_ref, column_ref, first, second):
    tile_row, column = tile_row_ref[0], column_ref[0]
    odd = (column & 1) == 1
    for row in range(0, ROWS, 8):
        lane = lax.broadcasted_iota(jnp.int32, (8, TILE), 1)
        to_right = [jnp.zeros((8, TILE), F32) for _ in range(PACKS)]
        to_left = [jnp.zeros((8, TILE), F32) for _ in range(PACKS)]
        for p in range(PLANES):
            if row < HALO:
                value = jnp.where(tile_row > 0, top[p, pl.ds(row, 8), :], 0.0)
            elif row < HALO + TILE:
                value = planes[p, pl.ds(row - HALO, 8), :]
            else:
                value = jnp.where(tile_row < ACROSS - 1, bottom[p, pl.ds(row - HALO - TILE, 8), :], 0.0)
            _, start, packs = slot(p)
            left = pltpu.roll(value, start, 1) if start else value
            right = pltpu.roll(value, (start + HALO) % TILE, 1)
            for pack in packs:
                at = lane + TILE * pack
                here = (at >= HALO * p) & (at < HALO * (p + 1))
                to_left[pack] = jnp.where(here, left, to_left[pack])
                to_right[pack] = jnp.where(here, right, to_right[pack])
        for pack in range(PACKS):
            first[pack, pl.ds(row, 8), :] = jnp.where(odd, to_left[pack], to_right[pack])
            second[pack, pl.ds(row, 8), :] = jnp.where(odd, to_right[pack], to_left[pack])


def chunk_rows(half):
    return [HALO + MAIN * half + 8 * k for k in range(8)] + ([8, 16], [ROWS - 24, ROWS - 16])[half]


def chunk_out(out, field, first=0):
    lane = lax.broadcasted_iota(jnp.int32, (8, TILE), 1)
    for c in range(RING):
        z, rows = c // 2, chunk_rows(c % 2)
        for k, row in enumerate(rows):
            out[c, pl.ds(first + 8 * k, 8), :] = field[z, 0, pl.ds(row, 8), :]
        for slot in range(3):
            packed = jnp.zeros((8, TILE), F32)
            for j, k in enumerate(range(slot, 10, 3)):
                value = pltpu.roll(field[z, 1, pl.ds(rows[k], 8), :], (SIDE + 32 * j) % TILE, 1)
                packed = jnp.where((lane >= 32 * j) & (lane < 32 * (j + 1)), value, packed)
            out[c, pl.ds(first + FULL + 8 * slot, 8), :] = packed


def three(own, halo, lane):
    own64, halo64 = pltpu.roll(own, 64, 1), pltpu.roll(halo, 64, 1)
    middle = jnp.where(lane < 32, halo, jnp.where(lane < 64, halo64, own64))
    last = jnp.where(lane < 64, own64, jnp.where(lane < 96, halo64, halo))
    return own, middle, last


def packed_gases(own0, halo0, own1, halo1, lane):
    own64, halo64 = pltpu.roll(own1, 64, 1), pltpu.roll(halo1, 64, 1)
    middle = jnp.where(lane < 32, halo0, jnp.where(lane < 64, halo64, own64))
    last = jnp.where(lane < 64, own64, jnp.where(lane < 96, halo64, halo0))
    return own0, middle, last


def sum_of_gases(tiles, lane):
    low = jnp.where(lane < 64, tiles[1], tiles[2])
    high = jnp.where(lane < 64, tiles[2], tiles[1])
    return tiles[0] + pltpu.roll(high, 64, 1), low + pltpu.roll(low, 64, 1)


def chunk_in(t4, chunks, change):
    lane = lax.broadcasted_iota(jnp.int32, (8, TILE), 1)
    for c in range(RING):
        z, rows = c // 2, chunk_rows(c % 2)
        sides = [change(chunks[c, pl.ds(FULL + 8 * k, 8), :]) for k in range(3)]
        for k, row in enumerate(rows):
            own = change(chunks[c, pl.ds(8 * k, 8), :])
            halo = pltpu.roll(sides[k % 3], (TILE - SIDE - 32 * (k // 3)) % TILE, 1)
            for t, value in enumerate(three(own, halo, lane)):
                t4[z, t, pl.ds(row, 8), :] = value


def own_chunk(me, out, layer):
    lane = lax.broadcasted_iota(jnp.int32, (8, TILE), 1)
    half = me[0] & 1
    low, high = chunk_rows(0), chunk_rows(1)
    rows = [pl.multiple_of(a + (b - a) * half, 8) for a, b in zip(low, high)]
    for k, row in enumerate(rows):
        out[pl.ds(8 * k, 8), :] = layer[0, pl.ds(row, 8), :]
    for slot_of in range(3):
        packed = jnp.zeros((8, TILE), F32)
        for j, k in enumerate(range(slot_of, 10, 3)):
            value = pltpu.roll(layer[1, pl.ds(rows[k], 8), :], (SIDE + 32 * j) % TILE, 1)
            packed = jnp.where((lane >= 32 * j) & (lane < 32 * (j + 1)), value, packed)
        out[pl.ds(FULL + 8 * slot_of, 8), :] = packed


def turn(me, k):
    return (me[0] + k) & 3


def send_chunks(me, chunks, outs):
    for k, out in enumerate(outs):
        out[...] = chunks[turn(me, k)]


def gather_chunks(me, chunks, parts):
    for k, part in zip(BACK, parts):
        chunks[turn(me, RING - k)] = part[...]


def fourth(value):
    square = value * value
    return square * square


def to_left_of(tiles, t, lane):
    return pltpu.roll(jnp.where(lane == TILE - 1, tiles[t - 1], tiles[t]), 1, 1)


def to_right_of(tiles, t, lane):
    return pltpu.roll(jnp.where(lane == 0, tiles[(t + 1) % 3], tiles[t]), TILE - 1, 1)


def each_step(first, last, body):
    for r in range(first, last, STEP):
        body(r)


def solve(step, a, q, t4, sp, start, now, old):
    first, last = 8 * step, ROWS - 8 * step

    def source(r):
        for z in range(2):
            for t in range(3):
                weight = q[z, t, pl.ds(r, STEP), :]
                value = weight * t4[z, t, pl.ds(r, STEP), :]
                sp[z, t, pl.ds(r, STEP), :] = jnp.where(weight > 0.0, value, 0.0)

    each_step(first, last, source)
    before, src = None, start
    for sweep, (keep, push) in enumerate(sweep_weights()):
        dst = old if sweep % 2 == 0 else now

        def body(r, src=src, dst=dst, before=before, keep=keep, push=push):
            lane = lax.broadcasted_iota(jnp.int32, (STEP, TILE), 1)
            rows = pl.ds(r, STEP)
            own = [[src[z, t, pl.ds(r + PAD, STEP), :] for t in range(3)] for z in range(2)]
            for z in range(2):
                for t in range(3):
                    here = own[z][t]
                    total = sp[z, t, rows, :] + a[0, z, t, rows, :] * own[1 - z][t]
                    total += a[1, z, t, rows, :] * src[z, t, pl.ds(r + PAD - 1, STEP), :]
                    total += a[2, z, t, rows, :] * src[z, t, pl.ds(r + PAD + 1, STEP), :]
                    total += a[3, z, t, rows, :] * to_left_of(own[z], t, lane)
                    total += a[4, z, t, rows, :] * to_right_of(own[z], t, lane)
                    value = (1.0 + keep - push) * here + push * total
                    if before is not None:
                        value -= keep * before[z, t, pl.ds(r + PAD, STEP), :]
                    dst[z, t, pl.ds(r + PAD, STEP), :] = value

        each_step(first, last, body)
        before, src = src, dst


def absorb(kap, now, out):
    lane = lax.broadcasted_iota(jnp.int32, (STEP, TILE), 1)

    def body(r):
        for z in range(2):
            rows = pl.ds(r + PAD, STEP)
            tiles = [kap[z, t, rows, :] * now[z, t, rows, :] for t in range(3)]
            for l, value in enumerate(sum_of_gases(tiles, lane)):
                out[z, l, pl.ds(r, STEP), :] = value

    each_step(8, ROWS - 8, body)


def first_kernel(planes, top, bottom, first, second, me, tile_row_ref, column_ref, *refs):
    a, q, kap, now, held, *outs = refs[: 5 + RING]
    tis, sp, t4, old, begin, shared, sums = refs[5 + RING :]
    tile_row, column = tile_row_ref[0], column_ref[0]
    odd = (column & 1) == 1

    def own_rows(p, row):
        if row < HALO:
            return jnp.where(tile_row > 0, top[p, pl.ds(row, 8), :], 0.0)
        if row < HALO + TILE:
            return planes[p, pl.ds(row - HALO, 8), :]
        return jnp.where(tile_row < ACROSS - 1, bottom[p, pl.ds(row - HALO - TILE, 8), :], 0.0)

    for row in range(0, ROWS, 8):
        lane = lax.broadcasted_iota(jnp.int32, (8, TILE), 1)
        got = [(first[pack, pl.ds(row, 8), :], second[pack, pl.ds(row, 8), :]) for pack in range(PACKS)]
        lefts = [jnp.where(column > 0, jnp.where(odd, f, s), 0.0) for f, s in got]
        rights = [jnp.where(column < ACROSS - 1, jnp.where(odd, s, f), 0.0) for f, s in got]
        halos = []
        for p in range(PLANES):
            pack, start, packs = slot(p)
            left, right = lefts[pack], rights[pack]
            if len(packs) > 1:
                left = jnp.where(lane >= start, left, lefts[pack + 1])
                right = jnp.where(lane >= start, right, rights[pack + 1])
            left = pltpu.roll(left, (2 * TILE - HALO - start) % TILE, 1)
            right = pltpu.roll(right, TILE - start, 1) if start else right
            halos.append(jnp.where(lane < HALO, right, jnp.where(lane >= TILE - HALO, left, 0.0)))
        for f, (dst, pad) in enumerate(((kap, PAD), (q, 0), (begin, PAD))):
            for z in range(2):
                p0, p1 = 4 * f + z, 4 * f + 2 + z
                tiles = packed_gases(own_rows(p0, row), halos[p0], own_rows(p1, row), halos[p1], lane)
                for t, value in enumerate(tiles):
                    dst[z, t, pl.ds(row + pad, 8), :] = value
        for p in range(12, PLANES):
            own = own_rows(p, row)
            tis[p - 12, 0, pl.ds(row, 8), :] = own
            tis[p - 12, 1, pl.ds(row, 8), :] = halos[p]
            if p < 14:
                for t, value in enumerate(three(fourth(own), fourth(halos[p]), lane)):
                    t4[p - 12, t, pl.ds(row, 8), :] = value

    own_chunk(me, held.at[0], tis.at[me[0] >> 1])
    own_chunk(me, held.at[1], tis.at[2])
    own_chunk(me, held.at[2], tis.at[3])

    def halves(r):
        lane = lax.broadcasted_iota(jnp.int32, (STEP, TILE), 1)
        rows, padded = pl.ds(r, STEP), pl.ds(r + PAD, STEP)
        for z in range(2):
            own = [kap[z, t, padded, :] for t in range(3)]
            for l, value in enumerate(sum_of_gases([own[t] * q[z, t, rows, :] for t in range(3)], lane)):
                shared[z, l, rows, :] = value
            for t in range(3):
                old[z, t, padded, :] = 1.0 / (own[t] + kap[z, t, pl.ds(r + PAD + 1, STEP), :])
                sp[z, t, rows, :] = 1.0 / (own[t] + to_right_of(own, t, lane))

    each_step(0, ROWS, halves)

    def coefficients(r):
        lane = lax.broadcasted_iota(jnp.int32, (STEP, TILE), 1)
        rows, padded = pl.ds(r, STEP), pl.ds(r + PAD, STEP)
        own = [[kap[z, t, padded, :] for t in range(3)] for z in range(2)]
        between = [1.0 / (own[0][t] + own[1][t]) for t in range(3)]
        for z in range(2):
            to_right = [sp[z, t, rows, :] for t in range(3)]
            for t in range(3):
                here = own[z][t]
                to_left = to_left_of(to_right, t, lane)
                to_up = old[z, t, pl.ds(r + PAD - 1, STEP), :]
                couplings = [between[t], to_up, old[z, t, padded, :], to_left, to_right[t]]
                diagonal = 1.5 * here + 1.0 / here
                for coupling in couplings:
                    diagonal += coupling
                inverse = 1.0 / diagonal
                for f, coupling in enumerate(couplings):
                    a[f, z, t, rows, :] = jnp.where(here > 0.0, coupling * inverse, 0.0)
                weight = 6.0 * here * q[z, t, rows, :] * inverse
                q[z, t, rows, :] = jnp.where(here > 0.0, weight, 0.0)

    each_step(0, ROWS, coefficients)
    chunk_out(sums, shared, CHUNK)
    solve(0, a, q, t4, sp, begin, now, old)
    absorb(kap, now, shared)
    chunk_out(sums, shared)
    send_chunks(me, sums, outs)


def next_kernel(a, q, kap, start, *refs):
    parts, me = refs[:RING], refs[RING]
    now, *outs = refs[RING + 1 : 2 * RING + 2]
    sp, t4, old, shared, sums = refs[2 * RING + 2 :]
    gather_chunks(me, sums, parts)
    chunk_in(t4, sums, fourth)
    solve(1, a, q, t4, sp, start, now, old)
    absorb(kap, now, shared)
    chunk_out(sums, shared)
    send_chunks(me, sums, outs)


def last_kernel(a, q, kap, start, *refs):
    parts, me = refs[:RING], refs[RING]
    now, *outs = refs[RING + 1 : 2 * RING + 2]
    sp, t4, old, sums = refs[2 * RING + 2 :]
    gather_chunks(me, sums, parts)
    chunk_in(t4, sums, fourth)
    solve(2, a, q, t4, sp, start, now, old)
    lane = lax.broadcasted_iota(jnp.int32, (MAIN, TILE), 1)
    for c in range(RING):
        z, half = c // 2, c % 2
        rows = pl.ds(PAD + HALO + MAIN * half, MAIN)
        tiles = [now[z, t, rows, :] for t in range(3)]
        taken = [kap[z, t, rows, :] * tiles[t] for t in range(3)]
        sums[c, pl.ds(0, MAIN), :] = sum_of_gases(taken, lane)[0]
    for k, out in enumerate(outs):
        out[...] = sums[turn(me, k), pl.ds(0, MAIN), :]


def radiation_kernel(now, radiation):
    lane = lax.broadcasted_iota(jnp.int32, (TILE, TILE), 1)
    for z in range(2):
        tiles = [now[z, t, pl.ds(PAD + HALO, TILE), :] for t in range(3)]
        radiation[0, 0, z] = tiles[0]
        radiation[1, 0, z] = pltpu.roll(jnp.where(lane < 64, tiles[2], tiles[1]), 64, 1)


def final_kernel(*refs):
    parts, me, out = refs[:RING], refs[RING], refs[RING + 1]
    gather_chunks(me, out, parts)


def corrected(current, earlier, inertia, source, emitted, taken):
    mismatch = inertia * (current - earlier) + 4.0 * emitted * fourth(current) - taken - source
    slope = inertia + 16.0 * emitted * (current * current * current)
    return jnp.where(inertia > 0.0, current - mismatch / slope, 0.0)


def call(kernel, outs, scratch=(), space=pltpu.VMEM, cost=None):
    def run(*args):
        return pl.pallas_call(
            kernel,
            out_shape=[jax.ShapeDtypeStruct(dims, F32) for dims in outs],
            in_specs=[
                pl.BlockSpec(memory_space=pltpu.SMEM if array.dtype == jnp.int32 else space) for array in args
            ],
            out_specs=[pl.BlockSpec(memory_space=pltpu.VMEM)] * len(outs),
            scratch_shapes=[pltpu.VMEM(s, F32) if isinstance(s, tuple) else s for s in scratch],
            compiler_params=pltpu.CompilerParams(vmem_limit_bytes=VMEM_LIMIT),
            cost_estimate=cost and pl.CostEstimate(flops=0, bytes_accessed=cost, transcendentals=0),
        )(*args)

    return run


FIELD = (2, 3, ROWS, TILE)
PADDED = (2, 3, ROWS + 2 * PAD, TILE)
SHARED = (2, 2, ROWS, TILE)
OUT_TURNS = (2, 3, 1)
BACK = (0, 3, 1, 2)


def along_y(array, by):
    pairs = [(4 * z + y, 4 * z + (y + by) % 4) for z in range(4) for y in range(4)]
    return lax.ppermute(array, "gas", pairs)


def along_z(array, by):
    pairs = [(4 * z + y, 4 * ((z + by) % 4) + y) for z in range(4) for y in range(4)]
    return lax.ppermute(array, "gas", pairs)


def sum_over_gas(parts):
    total = parts[0]
    for k in OUT_TURNS:
        total = total + along_y(parts[k], k)
    parts = [along_z(total, k) for k in (3, 1, 2)]
    return total + parts[0] + parts[1] + parts[2]


def spread(chunk):
    return [along_y(chunk, k) if k else chunk for k in BACK]


def on_device(*inputs):
    kelvin, inertia, source, extinction, fractions, irradiance = inputs
    own = (extinction, fractions, irradiance, kelvin, inertia, source)
    own = [pltpu.with_memory_space_constraint(array, pltpu.HBM) for array in own]
    devices = lax.axis_size("space")
    me = (lax.axis_index("gas") & 3).reshape(1)
    place = lax.axis_index("space")
    at = ((place >> 2).reshape(1), (place & 3).reshape(1))
    sems = pltpu.SemaphoreType.DMA((18,))
    up, down = call(edge_kernel, [(PLANES, HALO, TILE)] * 2, [sems], space=pltpu.HBM)(*own, me)
    (planes,) = call(load_kernel, [(PLANES, TILE, TILE)], [sems], space=pltpu.HBM, cost=4000000)(*own, me)
    ring = [(i, (i + ACROSS) % devices) for i in range(devices)]
    top = lax.ppermute(up, "space", ring)
    bottom = lax.ppermute(down, "space", [(j, i) for i, j in ring])
    first, second = call(pack_y_kernel, [(PACKS, ROWS, TILE)] * 2)(planes, top, bottom, *at)
    first = lax.ppermute(first, "space", [(i, i ^ 1) for i in range(devices)])
    swaps = (0, 2, 1, 3)
    second = lax.ppermute(second, "space", [(i, i - i % ACROSS + swaps[i % ACROSS]) for i in range(devices)])
    two = (2 * CHUNK, TILE)
    a, q, kap, now, held, *parts = call(
        first_kernel,
        [(5,) + FIELD, FIELD, PADDED, PADDED, (3, CHUNK, TILE)] + [two] * RING,
        [(4, 2, ROWS, TILE), FIELD, FIELD, PADDED, PADDED, SHARED, (RING,) + two],
    )(planes, top, bottom, first, second, me, *at)
    total = sum_over_gas(parts)
    taken, emitted = total[:CHUNK], total[CHUNK:]
    earlier, inertia, source = held[0], held[1], held[2]
    current = corrected(earlier, earlier, inertia, source, emitted, taken)
    one = (CHUNK, TILE)
    now, *parts = call(
        next_kernel, [PADDED] + [one] * RING, [FIELD, FIELD, PADDED, SHARED, (RING,) + one]
    )(a, q, kap, now, *spread(current), me)
    current = corrected(current, earlier, inertia, source, emitted, sum_over_gas(parts))
    now, *parts = call(
        last_kernel,
        [PADDED] + [(MAIN, TILE)] * RING,
        [FIELD, FIELD, PADDED, (RING,) + one],
    )(a, q, kap, now, *spread(current), me)
    (radiation,) = call(radiation_kernel, [(2, 1, 2, TILE, TILE)], cost=4000000)(now)
    rest = (value[:MAIN] for value in (current, earlier, inertia, source, emitted))
    current = corrected(*rest, sum_over_gas(parts))
    (final,) = call(final_kernel, [(RING, MAIN, TILE)])(*spread(current), me)
    return final.reshape(1, 2, TILE, TILE), radiation


def solution(mesh):
    placed = (
        P("space", None, None, None),
        P("space", None, None, None),
        P("space", None, None, None),
        P("gas", "space", None, None, None),
        P("gas", "space", None, None, None),
        P("gas", "space", None, None, None),
    )
    return jax.shard_map(
        on_device,
        mesh=mesh,
        in_specs=placed,
        out_specs=(P("space", None, None, None), P("gas", "space", None, None, None)),
        check_vma=False,
    )
```

```python
import functools

import jax
import jax.numpy as jnp
from jax import lax
from jax.experimental import pallas as pl
from jax.experimental.pallas import tpu as pltpu
from jax.sharding import PartitionSpec as P

SWEEPS = 8
OUTER = 3
LOW_BOUND = 0.05
HIGH_BOUND = 2.0

TILE = 128
HALO = SWEEPS * OUTER
ROWS = TILE + 2 * HALO
PAD = 8
STEP = 8
PLANES = 16
PACKS = 3
ACROSS = 4
RING = 4
MAIN = 64
FULL = 80
CHUNK = 104
SIDE = 16
VMEM_LIMIT = 16 * 1024 * 1024
F32 = jnp.float32


def sweep_weights():
    theta_mid = (HIGH_BOUND + LOW_BOUND) / 2.0
    delta_half = (HIGH_BOUND - LOW_BOUND) / 2.0
    sigma_ratio = theta_mid / delta_half
    rho_now = 1.0 / sigma_ratio
    weights = [(0.0, 1.0 / theta_mid)]
    for _ in range(SWEEPS - 1):
        rho_next = 1.0 / (2.0 * sigma_ratio - rho_now)
        weights.append((rho_next * rho_now, 2.0 * rho_next / delta_half))
        rho_now = rho_next
    return weights


def field_sources(refs, me):
    sources = [(refs[f].at[gas, 0], 4 * f + 2 * gas, 2) for f in range(3) for gas in range(2)]
    sources.append((refs[3].at[0], 12, 2))
    layer = me[0] >> 1
    return sources + [(refs[4 + f].at[0, pl.ds(layer, 1)], 14 + f, 1) for f in range(2)]


def copy_rows(refs, me, parts, sems):
    copies = []
    for source, first, layers in field_sources(refs, me):
        for row, count, out in parts:
            copies.append(
                pltpu.make_async_copy(
                    source.at[:, pl.ds(row, count), :], out.at[pl.ds(first, layers)], sems.at[len(copies)]
                )
            )
    for copy in copies:
        copy.start()
    for copy in copies:
        copy.wait()


def edge_kernel(*refs):
    me, up, down, sems = refs[6:]
    copy_rows(refs[:6], me, ((TILE - HALO, HALO, up), (0, HALO, down)), sems)


def load_kernel(*refs):
    me, planes, sems = refs[6:]
    copy_rows(refs[:6], me, ((0, TILE, planes),), sems)


def slot(p):
    pack, lane = divmod(HALO * p, TILE)
    return pack, lane, [pack] if lane + HALO <= TILE else [pack, pack + 1]


def pack_y_kernel(planes, top, bottom, tile_row_ref, column_ref, first, second):
    tile_row, column = tile_row_ref[0], column_ref[0]
    odd = (column & 1) == 1
    for row in range(0, ROWS, 8):
        lane = lax.broadcasted_iota(jnp.int32, (8, TILE), 1)
        to_right = [jnp.zeros((8, TILE), F32) for _ in range(PACKS)]
        to_left = [jnp.zeros((8, TILE), F32) for _ in range(PACKS)]
        for p in range(PLANES):
            if row < HALO:
                value = jnp.where(tile_row > 0, top[p, pl.ds(row, 8), :], 0.0)
            elif row < HALO + TILE:
                value = planes[p, pl.ds(row - HALO, 8), :]
            else:
                value = jnp.where(tile_row < ACROSS - 1, bottom[p, pl.ds(row - HALO - TILE, 8), :], 0.0)
            _, start, packs = slot(p)
            left = pltpu.roll(value, start, 1) if start else value
            right = pltpu.roll(value, (start + HALO) % TILE, 1)
            for pack in packs:
                at = lane + TILE * pack
                here = (at >= HALO * p) & (at < HALO * (p + 1))
                to_left[pack] = jnp.where(here, left, to_left[pack])
                to_right[pack] = jnp.where(here, right, to_right[pack])
        for pack in range(PACKS):
            first[pack, pl.ds(row, 8), :] = jnp.where(odd, to_left[pack], to_right[pack])
            second[pack, pl.ds(row, 8), :] = jnp.where(odd, to_right[pack], to_left[pack])


def chunk_rows(half):
    return [HALO + MAIN * half + 8 * k for k in range(8)] + ([8, 16], [ROWS - 24, ROWS - 16])[half]


def chunk_out(out, field, first=0):
    lane = lax.broadcasted_iota(jnp.int32, (8, TILE), 1)
    for c in range(RING):
        z, rows = c // 2, chunk_rows(c % 2)
        for k, row in enumerate(rows):
            out[c, pl.ds(first + 8 * k, 8), :] = field[z, 0, pl.ds(row, 8), :]
        for slot in range(3):
            packed = jnp.zeros((8, TILE), F32)
            for j, k in enumerate(range(slot, 10, 3)):
                value = pltpu.roll(field[z, 1, pl.ds(rows[k], 8), :], (SIDE + 32 * j) % TILE, 1)
                packed = jnp.where((lane >= 32 * j) & (lane < 32 * (j + 1)), value, packed)
            out[c, pl.ds(first + FULL + 8 * slot, 8), :] = packed


def three(own, halo, lane):
    own64, halo64 = pltpu.roll(own, 64, 1), pltpu.roll(halo, 64, 1)
    middle = jnp.where(lane < 32, halo, jnp.where(lane < 64, halo64, own64))
    last = jnp.where(lane < 64, own64, jnp.where(lane < 96, halo64, halo))
    return own, middle, last


def packed_gases(own0, halo0, own1, halo1, lane):
    own64, halo64 = pltpu.roll(own1, 64, 1), pltpu.roll(halo1, 64, 1)
    middle = jnp.where(lane < 32, halo0, jnp.where(lane < 64, halo64, own64))
    last = jnp.where(lane < 64, own64, jnp.where(lane < 96, halo64, halo0))
    return own0, middle, last


def sum_of_gases(tiles, lane):
    low = jnp.where(lane < 64, tiles[1], tiles[2])
    high = jnp.where(lane < 64, tiles[2], tiles[1])
    return tiles[0] + pltpu.roll(high, 64, 1), low + pltpu.roll(low, 64, 1)


def chunk_in(t4, chunks, change):
    lane = lax.broadcasted_iota(jnp.int32, (8, TILE), 1)
    for c in range(RING):
        z, rows = c // 2, chunk_rows(c % 2)
        sides = [change(chunks[c, pl.ds(FULL + 8 * k, 8), :]) for k in range(3)]
        for k, row in enumerate(rows):
            own = change(chunks[c, pl.ds(8 * k, 8), :])
            halo = pltpu.roll(sides[k % 3], (TILE - SIDE - 32 * (k // 3)) % TILE, 1)
            for t, value in enumerate(three(own, halo, lane)):
                t4[z, t, pl.ds(row, 8), :] = value


def own_chunk(me, out, layer):
    lane = lax.broadcasted_iota(jnp.int32, (8, TILE), 1)
    half = me[0] & 1
    low, high = chunk_rows(0), chunk_rows(1)
    rows = [pl.multiple_of(a + (b - a) * half, 8) for a, b in zip(low, high)]
    for k, row in enumerate(rows):
        out[pl.ds(8 * k, 8), :] = layer[0, pl.ds(row, 8), :]
    for slot_of in range(3):
        packed = jnp.zeros((8, TILE), F32)
        for j, k in enumerate(range(slot_of, 10, 3)):
            value = pltpu.roll(layer[1, pl.ds(rows[k], 8), :], (SIDE + 32 * j) % TILE, 1)
            packed = jnp.where((lane >= 32 * j) & (lane < 32 * (j + 1)), value, packed)
        out[pl.ds(FULL + 8 * slot_of, 8), :] = packed


def turn(me, k):
    return (me[0] + k) & 3


def send_chunks(me, chunks, outs):
    for k, out in enumerate(outs):
        out[...] = chunks[turn(me, k)]


def gather_chunks(me, chunks, parts):
    for k, part in zip(BACK, parts):
        chunks[turn(me, RING - k)] = part[...]


def fourth(value):
    square = value * value
    return square * square


def to_left_of(tiles, t, lane):
    return pltpu.roll(jnp.where(lane == TILE - 1, tiles[t - 1], tiles[t]), 1, 1)


def to_right_of(tiles, t, lane):
    return pltpu.roll(jnp.where(lane == 0, tiles[(t + 1) % 3], tiles[t]), TILE - 1, 1)


def each_step(first, last, body):
    for r in range(first, last, STEP):
        body(r)


def solve(step, a, q, t4, sp, start, now, old):
    first, last = 8 * step, ROWS - 8 * step

    def source(r):
        for z in range(2):
            for t in range(3):
                weight = q[z, t, pl.ds(r, STEP), :]
                value = weight * t4[z, t, pl.ds(r, STEP), :]
                sp[z, t, pl.ds(r, STEP), :] = jnp.where(weight > 0.0, value, 0.0)

    each_step(first, last, source)
    before, src = None, start
    for sweep, (keep, push) in enumerate(sweep_weights()):
        dst = old if sweep % 2 == 0 else now

        def body(r, src=src, dst=dst, before=before, keep=keep, push=push):
            lane = lax.broadcasted_iota(jnp.int32, (STEP, TILE), 1)
            rows = pl.ds(r, STEP)
            own = [[src[z, t, pl.ds(r + PAD, STEP), :] for t in range(3)] for z in range(2)]
            for z in range(2):
                for t in range(3):
                    here = own[z][t]
                    total = sp[z, t, rows, :] + a[0, z, t, rows, :] * own[1 - z][t]
                    total += a[1, z, t, rows, :] * src[z, t, pl.ds(r + PAD - 1, STEP), :]
                    total += a[2, z, t, rows, :] * src[z, t, pl.ds(r + PAD + 1, STEP), :]
                    total += a[3, z, t, rows, :] * to_left_of(own[z], t, lane)
                    total += a[4, z, t, rows, :] * to_right_of(own[z], t, lane)
                    value = (1.0 + keep - push) * here + push * total
                    if before is not None:
                        value -= keep * before[z, t, pl.ds(r + PAD, STEP), :]
                    dst[z, t, pl.ds(r + PAD, STEP), :] = value

        each_step(first, last, body)
        before, src = src, dst


def absorb(kap, now, out):
    lane = lax.broadcasted_iota(jnp.int32, (STEP, TILE), 1)

    def body(r):
        for z in range(2):
            rows = pl.ds(r + PAD, STEP)
            tiles = [kap[z, t, rows, :] * now[z, t, rows, :] for t in range(3)]
            for l, value in enumerate(sum_of_gases(tiles, lane)):
                out[z, l, pl.ds(r, STEP), :] = value

    each_step(8, ROWS - 8, body)


def first_kernel(planes, top, bottom, first, second, me, tile_row_ref, column_ref, *refs):
    a, q, kap, now, held, *outs = refs[: 5 + RING]
    tis, sp, t4, old, begin, shared, sums = refs[5 + RING :]
    tile_row, column = tile_row_ref[0], column_ref[0]
    odd = (column & 1) == 1

    def own_rows(p, row):
        if row < HALO:
            return jnp.where(tile_row > 0, top[p, pl.ds(row, 8), :], 0.0)
        if row < HALO + TILE:
            return planes[p, pl.ds(row - HALO, 8), :]
        return jnp.where(tile_row < ACROSS - 1, bottom[p, pl.ds(row - HALO - TILE, 8), :], 0.0)

    for row in range(0, ROWS, 8):
        lane = lax.broadcasted_iota(jnp.int32, (8, TILE), 1)
        got = [(first[pack, pl.ds(row, 8), :], second[pack, pl.ds(row, 8), :]) for pack in range(PACKS)]
        lefts = [jnp.where(column > 0, jnp.where(odd, f, s), 0.0) for f, s in got]
        rights = [jnp.where(column < ACROSS - 1, jnp.where(odd, s, f), 0.0) for f, s in got]
        halos = []
        for p in range(PLANES):
            pack, start, packs = slot(p)
            left, right = lefts[pack], rights[pack]
            if len(packs) > 1:
                left = jnp.where(lane >= start, left, lefts[pack + 1])
                right = jnp.where(lane >= start, right, rights[pack + 1])
            left = pltpu.roll(left, (2 * TILE - HALO - start) % TILE, 1)
            right = pltpu.roll(right, TILE - start, 1) if start else right
            halos.append(jnp.where(lane < HALO, right, jnp.where(lane >= TILE - HALO, left, 0.0)))
        for f, (dst, pad) in enumerate(((kap, PAD), (q, 0), (begin, PAD))):
            for z in range(2):
                p0, p1 = 4 * f + z, 4 * f + 2 + z
                tiles = packed_gases(own_rows(p0, row), halos[p0], own_rows(p1, row), halos[p1], lane)
                for t, value in enumerate(tiles):
                    dst[z, t, pl.ds(row + pad, 8), :] = value
        for p in range(12, PLANES):
            own = own_rows(p, row)
            tis[p - 12, 0, pl.ds(row, 8), :] = own
            tis[p - 12, 1, pl.ds(row, 8), :] = halos[p]
            if p < 14:
                for t, value in enumerate(three(fourth(own), fourth(halos[p]), lane)):
                    t4[p - 12, t, pl.ds(row, 8), :] = value

    own_chunk(me, held.at[0], tis.at[me[0] >> 1])
    own_chunk(me, held.at[1], tis.at[2])
    own_chunk(me, held.at[2], tis.at[3])

    def halves(r):
        lane = lax.broadcasted_iota(jnp.int32, (STEP, TILE), 1)
        rows, padded = pl.ds(r, STEP), pl.ds(r + PAD, STEP)
        for z in range(2):
            own = [kap[z, t, padded, :] for t in range(3)]
            for l, value in enumerate(sum_of_gases([own[t] * q[z, t, rows, :] for t in range(3)], lane)):
                shared[z, l, rows, :] = value
            for t in range(3):
                old[z, t, padded, :] = 1.0 / (own[t] + kap[z, t, pl.ds(r + PAD + 1, STEP), :])
                sp[z, t, rows, :] = 1.0 / (own[t] + to_right_of(own, t, lane))

    each_step(0, ROWS, halves)

    def coefficients(r):
        lane = lax.broadcasted_iota(jnp.int32, (STEP, TILE), 1)
        rows, padded = pl.ds(r, STEP), pl.ds(r + PAD, STEP)
        own = [[kap[z, t, padded, :] for t in range(3)] for z in range(2)]
        between = [1.0 / (own[0][t] + own[1][t]) for t in range(3)]
        for z in range(2):
            to_right = [sp[z, t, rows, :] for t in range(3)]
            for t in range(3):
                here = own[z][t]
                to_left = to_left_of(to_right, t, lane)
                to_up = old[z, t, pl.ds(r + PAD - 1, STEP), :]
                couplings = [between[t], to_up, old[z, t, padded, :], to_left, to_right[t]]
                diagonal = 1.5 * here + 1.0 / here
                for coupling in couplings:
                    diagonal += coupling
                inverse = 1.0 / diagonal
                for f, coupling in enumerate(couplings):
                    a[f, z, t, rows, :] = jnp.where(here > 0.0, coupling * inverse, 0.0)
                weight = 6.0 * here * q[z, t, rows, :] * inverse
                q[z, t, rows, :] = jnp.where(here > 0.0, weight, 0.0)

    each_step(0, ROWS, coefficients)
    chunk_out(sums, shared, CHUNK)
    solve(0, a, q, t4, sp, begin, now, old)
    absorb(kap, now, shared)
    chunk_out(sums, shared)
    send_chunks(me, sums, outs)


def next_kernel(a, q, kap, start, *refs):
    parts, me = refs[:RING], refs[RING]
    now, *outs = refs[RING + 1 : 2 * RING + 2]
    sp, t4, old, shared, sums = refs[2 * RING + 2 :]
    gather_chunks(me, sums, parts)
    chunk_in(t4, sums, fourth)
    solve(1, a, q, t4, sp, start, now, old)
    absorb(kap, now, shared)
    chunk_out(sums, shared)
    send_chunks(me, sums, outs)


def last_kernel(a, q, kap, start, *refs):
    parts, me = refs[:RING], refs[RING]
    now, *outs = refs[RING + 1 : 2 * RING + 2]
    sp, t4, old, sums = refs[2 * RING + 2 :]
    gather_chunks(me, sums, parts)
    chunk_in(t4, sums, fourth)
    solve(2, a, q, t4, sp, start, now, old)
    lane = lax.broadcasted_iota(jnp.int32, (MAIN, TILE), 1)
    for c in range(RING):
        z, half = c // 2, c % 2
        rows = pl.ds(PAD + HALO + MAIN * half, MAIN)
        tiles = [now[z, t, rows, :] for t in range(3)]
        taken = [kap[z, t, rows, :] * tiles[t] for t in range(3)]
        sums[c, pl.ds(0, MAIN), :] = sum_of_gases(taken, lane)[0]
    for k, out in enumerate(outs):
        out[...] = sums[turn(me, k), pl.ds(0, MAIN), :]


def radiation_kernel(now, radiation):
    lane = lax.broadcasted_iota(jnp.int32, (TILE, TILE), 1)
    for z in range(2):
        tiles = [now[z, t, pl.ds(PAD + HALO, TILE), :] for t in range(3)]
        radiation[0, 0, z] = tiles[0]
        radiation[1, 0, z] = pltpu.roll(jnp.where(lane < 64, tiles[2], tiles[1]), 64, 1)


def final_kernel(*refs):
    parts, me, out = refs[:RING], refs[RING], refs[RING + 1]
    gather_chunks(me, out, parts)


def corrected(current, earlier, inertia, source, emitted, taken):
    mismatch = inertia * (current - earlier) + 4.0 * emitted * fourth(current) - taken - source
    slope = inertia + 16.0 * emitted * (current * current * current)
    return jnp.where(inertia > 0.0, current - mismatch / slope, 0.0)


def call(kernel, outs, scratch=(), space=pltpu.VMEM, cost=None):
    def run(*args):
        return pl.pallas_call(
            kernel,
            out_shape=[jax.ShapeDtypeStruct(dims, F32) for dims in outs],
            in_specs=[
                pl.BlockSpec(memory_space=pltpu.SMEM if array.dtype == jnp.int32 else space) for array in args
            ],
            out_specs=[pl.BlockSpec(memory_space=pltpu.VMEM)] * len(outs),
            scratch_shapes=[pltpu.VMEM(s, F32) if isinstance(s, tuple) else s for s in scratch],
            compiler_params=pltpu.CompilerParams(vmem_limit_bytes=VMEM_LIMIT),
            cost_estimate=cost and pl.CostEstimate(flops=0, bytes_accessed=cost, transcendentals=0),
        )(*args)

    return run


FIELD = (2, 3, ROWS, TILE)
PADDED = (2, 3, ROWS + 2 * PAD, TILE)
SHARED = (2, 2, ROWS, TILE)
OUT_TURNS = (2, 1, 3)
BACK = (0, 3, 1, 2)


def along_y(array, by):
    pairs = [(4 * z + y, 4 * z + (y + by) % 4) for z in range(4) for y in range(4)]
    return lax.ppermute(array, "gas", pairs)


def along_z(array, by):
    pairs = [(4 * z + y, 4 * ((z + by) % 4) + y) for z in range(4) for y in range(4)]
    return lax.ppermute(array, "gas", pairs)


def sum_over_gas(parts):
    total = parts[0]
    for k in OUT_TURNS:
        total = total + along_y(parts[k], k)
    parts = [along_z(total, k) for k in (3, 1, 2)]
    return total + parts[0] + parts[1] + parts[2]


def spread(chunk):
    return [along_y(chunk, k) if k else chunk for k in BACK]


def on_device(*inputs):
    kelvin, inertia, source, extinction, fractions, irradiance = inputs
    own = (extinction, fractions, irradiance, kelvin, inertia, source)
    own = [pltpu.with_memory_space_constraint(array, pltpu.HBM) for array in own]
    devices = lax.axis_size("space")
    me = (lax.axis_index("gas") & 3).reshape(1)
    place = lax.axis_index("space")
    at = ((place >> 2).reshape(1), (place & 3).reshape(1))
    sems = pltpu.SemaphoreType.DMA((18,))
    up, down = call(edge_kernel, [(PLANES, HALO, TILE)] * 2, [sems], space=pltpu.HBM)(*own, me)
    (planes,) = call(load_kernel, [(PLANES, TILE, TILE)], [sems], space=pltpu.HBM, cost=4000000)(*own, me)
    ring = [(i, (i + ACROSS) % devices) for i in range(devices)]
    top = lax.ppermute(up, "space", ring)
    bottom = lax.ppermute(down, "space", [(j, i) for i, j in ring])
    first, second = call(pack_y_kernel, [(PACKS, ROWS, TILE)] * 2)(planes, top, bottom, *at)
    first = lax.ppermute(first, "space", [(i, i ^ 1) for i in range(devices)])
    swaps = (0, 2, 1, 3)
    second = lax.ppermute(second, "space", [(i, i - i % ACROSS + swaps[i % ACROSS]) for i in range(devices)])
    two = (2 * CHUNK, TILE)
    a, q, kap, now, held, *parts = call(
        first_kernel,
        [(5,) + FIELD, FIELD, PADDED, PADDED, (3, CHUNK, TILE)] + [two] * RING,
        [(4, 2, ROWS, TILE), FIELD, FIELD, PADDED, PADDED, SHARED, (RING,) + two],
    )(planes, top, bottom, first, second, me, *at)
    total = sum_over_gas(parts)
    taken, emitted = total[:CHUNK], total[CHUNK:]
    earlier, inertia, source = held[0], held[1], held[2]
    current = corrected(earlier, earlier, inertia, source, emitted, taken)
    one = (CHUNK, TILE)
    now, *parts = call(
        next_kernel, [PADDED] + [one] * RING, [FIELD, FIELD, PADDED, SHARED, (RING,) + one]
    )(a, q, kap, now, *spread(current), me)
    current = corrected(current, earlier, inertia, source, emitted, sum_over_gas(parts))
    now, *parts = call(
        last_kernel,
        [PADDED] + [(MAIN, TILE)] * RING,
        [FIELD, FIELD, PADDED, (RING,) + one],
    )(a, q, kap, now, *spread(current), me)
    (radiation,) = call(radiation_kernel, [(2, 1, 2, TILE, TILE)], cost=4000000)(now)
    rest = (value[:MAIN] for value in (current, earlier, inertia, source, emitted))
    current = corrected(*rest, sum_over_gas(parts))
    (final,) = call(final_kernel, [(RING, MAIN, TILE)])(*spread(current), me)
    return final.reshape(1, 2, TILE, TILE), radiation


def solution(mesh):
    placed = (
        P("space", None, None, None),
        P("space", None, None, None),
        P("space", None, None, None),
        P("gas", "space", None, None, None),
        P("gas", "space", None, None, None),
        P("gas", "space", None, None, None),
    )
    return jax.shard_map(
        on_device,
        mesh=mesh,
        in_specs=placed,
        out_specs=(P("space", None, None, None), P("gas", "space", None, None, None)),
        check_vma=False,
    )
```
